512 devices in a mesh: pair: 64 (over z, y), band: 8 (over x, core).
Axes of the slice: x: 4, y: 4, z: 16, core: 2. Of those that a mesh axis runs over, the one named last changes fastest.
Arguments:
- spectrum: bfloat16 [4096, 98304], P('band', 'pair'), may hold values from -6 to 6
- bessel_table: bfloat16 [4096, 512], P('band'), may hold values from -0.125 to 0.125
- interp_weights: bfloat16 [256, 8, 256, 512], P('pair', None, None, 'band'), may hold values from -0.09375 to 0.09375
- need_owner: int32 [256, 8], P('pair'), may hold values from 0 to 63, all different within a row; in each aligned block of 4 rows (0 to 3, 4 to 7, ...) at most 2 rows name the same one
- need_block: int32 [256, 8], P('pair'), may hold values from 0 to 11
Outputs:
- stress: float32 [256, 256, 128], P('pair', 'band')
The draws below stay inside these ranges and needn't reach their ends.
Inputs may be any that keep to these rules, and one draw needn't show every extreme that they name: `need_owner`: each row names 8 different owners; among the 4 rows of one index of pair no owner is named by more than 2 rows, a bound that some block reaches.
All inputs are finite; a program needn't handle non-finite values.
Results may differ from the reference program's by a relative error of at most 0.0003.
Values sent between devices are 32-bit elements; how exact they have to be, the bound alone decides.
A program may use at most 64 MiB of HBM per device.

```python
import math
import jax
import jax.numpy as jnp
import numpy as np
from jax import lax

R = 512
K = 4096
PB = 128
TRI = 256
NB = 8
BLK_DEV = 12
TILE_DEV = 4
KB = 512
NPAIR = 98304
BLOCKS = 768
TILES = 256
CAP = 2
N_PAIR = 64
N_BAND = 8


def set_ends(drawn, rng, least, largest):
    longest = drawn.shape.index(max(drawn.shape))
    spots = []
    for shift in (0, 1):
        where = [jax.random.randint(jax.random.fold_in(rng, axis), (), 0, length) for axis, length in enumerate(drawn.shape)]
        where[longest] = (where[longest] + shift) % drawn.shape[longest]
        spots.append(tuple(where))
    return drawn.at[spots[0]].set(least).at[spots[1]].set(largest)


def raised(drawn, own_key, source, target, blocks, factor):
    owner, partner = [(jnp.arange(drawn.shape[axis_at]) // (drawn.shape[axis_at] // blocks)).reshape([-1 if axis == axis_at else 1 for axis in range(drawn.ndim)]) for axis_at in (source, target)]
    chosen = jax.random.permutation(own_key, blocks)[partner]
    strong = (owner == chosen) | (owner == (partner + blocks // 2) % blocks)
    return jnp.where(strong, factor * drawn, drawn)


def block_scale(key, dims, split, smallest, largest):
    def one(axis_at, blocks):
        draws = jax.random.uniform(jax.random.fold_in(jax.random.fold_in(key, 6), axis_at), (blocks,), jnp.float32, smallest / len(split), largest / len(split))
        return jnp.repeat(jnp.exp(draws), dims[axis_at] // blocks).reshape((-1,) + (1,) * (len(dims) - axis_at - 1))

    loudness = one(*split[0])
    for cut in split[1:]:
        loudness = loudness * one(*cut)
    return loudness


def assign_block(stream_key, own, number, rows, amount, top, most, lean):
    sequence = jax.random.permutation(stream_key, amount)
    heavy_load, common = load_shares(amount, rows * top, most, lean, True), load_shares(amount, rows * top, most, lean, False)
    places = jnp.arange(amount)

    def named(tallies, offset_by):
        used = int((tallies > 0).sum())
        fixed = max(1, used // 4)
        shifted = fixed + (places - fixed + offset_by * (used - fixed)) % max(1, amount - fixed)
        return jnp.zeros((amount,), jnp.int32).at[sequence[jnp.where(places < fixed, places, shifted)]].set(jnp.asarray(tallies, jnp.int32))

    tallies = jnp.where(number % 4 == 0, named(heavy_load, number // 4), named(common, number - number // 4 - 1))
    mixed = jax.random.permutation(jax.random.fold_in(own, 3), amount)
    source_of, receiver = mixed[0:amount // 2 * 2:2], mixed[1:amount // 2 * 2:2]
    slack = jnp.minimum(tallies[source_of] - 1, most - tallies[receiver]) // 2
    slack = jnp.where((source_of == sequence[0]) | (receiver == sequence[0]) | (tallies[receiver] == 0), 0, jnp.maximum(slack, 0))
    shifted = jax.random.randint(jax.random.fold_in(own, 4), (amount // 2,), 0, 1 << 20) % (slack + 1)
    tallies = tallies.at[source_of].add(-shifted).at[receiver].add(shifted)
    members = jnp.searchsorted(jnp.cumsum(tallies), jnp.arange(rows * top), side="right").astype(jnp.int32)
    table = members.reshape(top, rows).T
    table = table[jax.random.permutation(jax.random.fold_in(own, 1), rows)]
    offset_by = jax.random.randint(jax.random.fold_in(own, 2), (rows, 1), 0, top)
    return jnp.take_along_axis(table, (jnp.arange(top)[None, :] + offset_by) % top, axis=1)


def load_shares(count, total, reach, slope, full):
    loads = [(1 << 20) // math.isqrt(rank ** slope) + 1 for rank in range(1, count + 1)]
    largest = reach if full else min(reach, max(-(-total // count), total * loads[0] // sum(loads)))
    least = 1 if total - largest >= count - 1 else 0
    counts, surplus = [largest] + [least] * (count - 1), total - largest - least * (count - 1)
    while surplus > 0:
        candidates = [i for i in range(1, count) if counts[i] < largest] or [i for i in range(1, count) if counts[i] < reach]
        mass, budget = sum([loads[i] for i in candidates]), surplus
        for i in candidates:
            more = min(reach - counts[i], max(1, budget * loads[i] // mass), surplus)
            counts[i] = counts[i] + more
            surplus = surplus - more
    return np.array(counts)


def noise(rng, dims, spread, bound, split=(), kind=jnp.bfloat16):
    array = jax.random.normal(rng, dims, jnp.float32) * spread
    if len(split) > 0:
        array = block_scale(rng, dims, split, -0.22, 0.18) * array
    return jnp.clip(array, min=-bound, max=bound).astype(kind)


def bell_draw_with(key, extent, spread, most, pieces, heavy, kind=jnp.bfloat16):
    drawn = spread * jax.random.normal(key, extent, jnp.float32)
    if pieces:
        drawn = drawn * block_scale(key, extent, pieces, -0.22, 0.18)
    return jnp.clip(raised(drawn, jax.random.fold_in(key, 3), *heavy), -most, most).astype(kind)


def setup_inputs(seed: int = 0) -> dict:
    seeds = jax.random.split(jax.random.key(seed), 6)
    spectrum = noise(seeds[0], (K, NPAIR), 1.0, 6.0, ((0, 8), (1, 64)))
    bessel_table = bell_draw_with(seeds[1], (K, R), K ** -0.5, 0.125, ((0, 8),), (0, 1, 8, 2.0))
    interp_weights = noise(seeds[2], (TILES, NB, TRI, R), (NB * R) ** -0.5, 0.09375, ((0, 64), (3, 8)))
    need_owner_keys = jax.random.split(jax.random.fold_in(seeds[3], 1), TILES // TILE_DEV)
    need_owner_turns = jax.random.permutation(jax.random.fold_in(seeds[3], 3), TILES // TILE_DEV)
    need_owner = jax.vmap(lambda own, number: assign_block(jax.random.fold_in(seeds[3], 2), own, number, TILE_DEV, N_PAIR, NB, CAP, 2))(need_owner_keys, need_owner_turns).reshape((TILES, NB))
    need_block = set_ends(jax.random.randint(seeds[4], (TILES, NB), 0, BLK_DEV), jax.random.fold_in(seeds[4], 1), 0, BLK_DEV - 1).astype(jnp.int32)
    return {"spectrum": spectrum, "bessel_table": bessel_table, "interp_weights": interp_weights, "need_owner": need_owner, "need_block": need_block}


def reference(spectrum, bessel_table, interp_weights, need_owner, need_block):
    table_bands = bessel_table.astype(jnp.float32).reshape(N_BAND, KB, R)
    spec_bands = spectrum.reshape(N_BAND, KB, NPAIR)

    def one_block(index):
        piece = lax.dynamic_slice_in_dim(spec_bands, index * PB, PB, 2).astype(jnp.float32)
        partial_value = jnp.einsum("bkr,bkp->brp", table_bands, piece)
        return jnp.sum(partial_value, axis=0)

    kernel = lax.map(one_block, jnp.arange(BLOCKS, dtype=jnp.int32))
    source = (need_owner * BLK_DEV + need_block).astype(jnp.int32)

    def one_tile(items):
        weights_tile, source_tile = items
        blocks = kernel[source_tile]
        return jnp.einsum("jtr,jrp->tp", weights_tile.astype(jnp.float32), blocks, precision=lax.Precision.HIGHEST)

    return lax.map(one_tile, (interp_weights, source))
```

```python
import functools

import jax
import jax.numpy as jnp
from jax import lax
from jax.experimental import pallas as pl
from jax.experimental.pallas import tpu as pltpu
from jax.sharding import PartitionSpec as P

PB = 128
NY = 4
CH = 16
MESH = pl.DeviceIdType.MESH
F32 = jnp.float32
BF16 = jnp.bfloat16


def kernel(
    sizes,
    table_in, spec_in, weights_in, owner_in, block_in,
    out,
    table, spec, weights, table_t, weights_t,
    part, core_in, band_in, ring, desk, picked, slots, blocks, share, share_in,
    wants, wants_s, place_s,
    load_sem, core_send, core_recv, x_send, x_recv, z_send, z_recv,
    want_send, want_recv, want_local, y_send, y_recv, f_send, f_recv,
):
    nx, nz, nq, nb, nt, nj, tri = sizes
    bands = 2 * nx
    half = nz // 2
    pair = lax.axis_index("pair")
    band = lax.axis_index("band")
    z, y = pair // NY, lax.rem(pair, NY)
    x, core = band // 2, lax.rem(band, 2)
    rows = tri // bands

    def x_peer(i):
        return (pair, lax.rem(x + i, nx) * 2 + core)

    def y_peer(i):
        return (z * NY + lax.rem(y + i, NY), band)

    def band_peer(i):
        return (pair, lax.rem(band + i, bands))

    sibling = (pair, x * 2 + 1 - core)
    up = (lax.rem(z + 1, nz) * NY + y, band)
    down = (lax.rem(z + nz - 1, nz) * NY + y, band)

    loads = [
        pltpu.make_async_copy(src, dst, load_sem.at[i])
        for i, (src, dst) in enumerate(((table_in, table), (spec_in, spec), (weights_in, weights)))
    ]
    for load in loads:
        load.start()

    barrier = pltpu.get_barrier_semaphore()
    partners = [band_peer(i) for i in range(1, bands)]
    partners += [y_peer(i) for i in range(1, NY)] + [up, down]
    for partner in partners:
        pl.semaphore_signal(barrier, inc=1, device_id=partner, device_id_type=MESH)

    loads[0].wait()
    turned = table[...].T
    for b in range(bands):
        for q in range(nq):
            at = b * nq * CH + q * CH
            table_t[q, b % 2, b // 2] = turned[at : at + CH]
    loads[1].wait()

    def hankel(q):
        left = table_t[q].reshape(bands * CH, table_t.shape[-1])
        product = jnp.dot(left, spec[...], preferred_element_type=F32)
        part[q] = product.reshape(2, nx, CH, nb * PB)

    def core_copy(q):
        return pltpu.make_async_remote_copy(
            part.at[q, 1 - core], core_in.at[q], core_send.at[q], core_recv.at[q],
            device_id=sibling, device_id_type=MESH,
        )

    def x_copy(q, i):
        return pltpu.make_async_remote_copy(
            part.at[q, core, lax.rem(x + i, nx)], band_in.at[q, nx - i],
            x_send.at[q, i], x_recv.at[q, nx - i],
            device_id=x_peer(i), device_id_type=MESH,
        )

    def across_cores(q):
        core_copy(q).wait_recv()
        part[q, core] = part[q, core] + core_in[q]
        for i in range(1, nx):
            x_copy(q, i).start()

    def own_rows(q):
        for i in range(1, nx):
            pltpu.make_async_copy(band_in.at[q, i], band_in.at[q, i], x_recv.at[q, i]).wait()
        total = part[q, core, x]
        for i in range(1, nx):
            total = total + band_in[q, i]
        for b in range(nb):
            ring[0, q, b] = total[:, b * PB : (b + 1) * PB]

    hankel(0)
    pl.semaphore_wait(barrier, len(partners))
    core_copy(0).start()

    lane = lax.broadcasted_iota(jnp.int32, (8, PB), 1)
    row = lax.broadcasted_iota(jnp.int32, (8, PB), 0)
    zero = jnp.zeros((8, PB), jnp.int32)

    def want_row(t, carry):
        first, second, count = carry
        for j in range(nj):
            hit = lane == owner_in[t, j]
            number = block_in[t, j]
            first = jnp.where(hit & (count == 0), number, first)
            second = jnp.where(hit & (count == 1), number, second)
            count = count + hit.astype(jnp.int32)
        return first, second, count

    first, second, _ = lax.fori_loop(0, nt, want_row, (zero, zero, zero))
    wants[0] = jnp.where(row == 0, first, jnp.where(row == 1, second, 0))

    def want_copy(i):
        return pltpu.make_async_remote_copy(
            wants.at[0], wants.at[NY - i], want_send.at[i], want_recv.at[NY - i],
            device_id=y_peer(i), device_id_type=MESH,
        )

    for i in range(1, NY):
        want_copy(i).start()

    for q in range(1, nq):
        hankel(q)
        core_copy(q).start()
        across_cores(q - 1)
    across_cores(nq - 1)

    def place_row(t, carry):
        for j in range(nj):
            who = owner_in[t, j]
            rank = jnp.int32(0)
            for u in range(nt - 1):
                for k in range(nj):
                    same = (owner_in[u, k] == who) & (u < t)
                    rank = rank + same.astype(jnp.int32)
            dz = lax.rem(z - who // NY + nz, nz)
            dy = lax.rem(lax.rem(who, NY) - y + NY, NY)
            spot = jnp.where(
                dz == 0, 0, jnp.where(dz == half, 1, jnp.where(dz < half, 2 * dz, 2 * (nz - dz) + 1))
            )
            place_s[t * nj + j] = (dy * nz + spot) * 2 + jnp.minimum(rank, 1)
        return carry

    lax.fori_loop(0, nt, place_row, 0)

    loads[2].wait()

    def turn(t, carry):
        weights_t[t] = weights[t].reshape(weights_t.shape[2], tri).T
        return carry

    lax.fori_loop(0, nt, turn, 0)

    for i in range(1, NY):
        pltpu.make_async_copy(wants.at[i], wants.at[i], want_recv.at[i]).wait()
    to_scalar = pltpu.make_async_copy(wants, wants_s, want_local)
    to_scalar.start()
    to_scalar.wait()

    def z_copy(way, d, q):
        here = d if way == 0 else lax.rem(nz - d, nz)
        there = d + 1 if way == 0 else nz - d - 1
        return pltpu.make_async_remote_copy(
            ring.at[here, q], ring.at[there, q], z_send.at[way], z_recv.at[way, d + 1, q],
            device_id=up if way == 0 else down, device_id_type=MESH,
        )

    def z_wait(way, d, q):
        here = d if way == 0 else nz - d
        pltpu.make_async_copy(ring.at[here, q], ring.at[here, q], z_recv.at[way, d, q]).wait()

    def y_copy(i, q, spot, count):
        at = pl.ds(spot * 2, count * 2)
        to = pl.ds((NY - i) * nz * 2 + spot * 2, count * 2)
        return pltpu.make_async_remote_copy(
            picked.at[q, i, at], slots.at[q, to], y_send, y_recv.at[q],
            device_id=y_peer(i), device_id_type=MESH,
        )

    def pick(q, spot, froms):
        for n, here in enumerate(froms):
            who = lax.rem(z - here + nz, nz) * NY + y
            desk[n] = ring[here, q]
            for i in range(NY):
                for s in range(2):
                    rows_of = desk[n, wants_s[i, s, who]]
                    if i == 0:
                        slots[q, (spot + n) * 2 + s] = rows_of
                    else:
                        picked[q, i, (spot + n) * 2 + s] = rows_of
        for i in range(1, NY):
            y_copy(i, q, spot, len(froms)).start()

    group = 2
    for g in range(nq // group):
        chunks = range(g * group, (g + 1) * group)
        for q in chunks:
            own_rows(q)
            z_copy(0, 0, q).start()
            z_copy(1, 0, q).start()
        for q in chunks:
            pick(q, 0, (0,))

        def step(d, carry):
            for q in chunks:
                for way in range(2):
                    z_wait(way, d, q)
                    z_copy(way, d, q).start()
            for q in chunks:
                pick(q, 2 * d, (d, nz - d))
            return carry

        lax.fori_loop(1, half - 1, step, 0)
        d = half - 1
        for q in chunks:
            for way in range(2):
                z_wait(way, d, q)
                if way == q % 2:
                    z_copy(way, d, q).start()
        for q in chunks:
            pick(q, 2 * d, (d, nz - d))
        for q in chunks:
            z_wait(q % 2, half, q)
            pick(q, 1, (half,))

    for q in range(nq):
        whole = slots.at[q, pl.ds(nz * 2, (NY - 1) * nz * 2)]
        pltpu.make_async_copy(whole, whole, y_recv.at[q]).wait()

    def tile(t, carry):
        for j in range(nj):
            place = place_s[t * nj + j]
            for q in range(nq):
                value = slots[q, place]
                high = value.astype(BF16)
                low = (value - high.astype(F32)).astype(BF16)
                at = (j * nq + q) * CH
                blocks[t, at : at + CH, :PB] = high
                blocks[t, at : at + CH, PB:] = low
        both = jnp.dot(weights_t[t], blocks[t], preferred_element_type=F32)
        total = both[:, :PB] + both[:, PB:]
        for b in range(bands):
            share[b, t] = total[b * rows : (b + 1) * rows]
        return carry

    lax.fori_loop(0, nt, tile, 0)

    def f_copy(i):
        return pltpu.make_async_remote_copy(
            share.at[lax.rem(band + i, bands)], share_in.at[bands - i], f_send.at[i], f_recv.at[bands - i],
            device_id=band_peer(i), device_id_type=MESH,
        )

    for i in range(1, bands):
        f_copy(i).start()
    total = share[band]
    for i in range(1, bands):
        pltpu.make_async_copy(share_in.at[i], share_in.at[i], f_recv.at[i]).wait()
        total = total + share_in[i]
    out[...] = total

    for q in range(nq):
        core_copy(q).wait_send()
        for i in range(1, nx):
            x_copy(q, i).wait_send()
    for i in range(1, NY):
        want_copy(i).wait_send()
    for i in range(1, bands):
        f_copy(i).wait_send()
    sent = (nz - 1) * nq // 2
    for way in range(2):
        for i in range(sent // nq):
            pltpu.make_async_copy(ring.at[i], ring.at[i], z_send.at[way]).wait()
        if sent % nq:
            some = ring.at[0, pl.ds(0, sent % nq)]
            pltpu.make_async_copy(some, some, z_send.at[way]).wait()
    whole = picked.at[:, pl.ds(1, NY - 1)]
    pltpu.make_async_copy(whole, whole, y_send).wait()


def shards(spectrum, bessel_table, interp_weights, need_owner, need_block):
    bands = lax.axis_size("band")
    nz = lax.axis_size("pair") // NY
    nx = bands // 2
    depth, radial = bessel_table.shape
    nb = spectrum.shape[1] // PB
    nt, nj, tri, local = interp_weights.shape
    nq = local // CH
    sizes = (nx, nz, nq, nb, nt, nj, tri)
    weights = jnp.swapaxes(interp_weights, 2, 3)
    dma = pltpu.SemaphoreType.DMA
    return pl.pallas_call(
        functools.partial(kernel, sizes),
        out_shape=jax.ShapeDtypeStruct((nt, tri // bands, PB), F32),
        in_specs=[pl.BlockSpec(memory_space=pl.ANY)] * 3
        + [pl.BlockSpec(memory_space=pltpu.SMEM)] * 2,
        out_specs=pl.BlockSpec(memory_space=pltpu.VMEM),
        scratch_shapes=[
            pltpu.VMEM((depth, radial), BF16),
            pltpu.VMEM(spectrum.shape, BF16),
            pltpu.VMEM(weights.shape, BF16),
            pltpu.VMEM((nq, 2, nx, CH, depth), BF16),
            pltpu.VMEM((nt, tri, nj * local), BF16),
            pltpu.VMEM((nq, 2, nx, CH, nb * PB), F32),
            pltpu.VMEM((nq, nx, CH, nb * PB), F32),
            pltpu.VMEM((nq, nx, CH, nb * PB), F32),
            pltpu.VMEM((nz, nq, nb, CH, PB), F32),
            pltpu.VMEM((2, nb, CH, PB), F32),
            pltpu.VMEM((nq, NY, nz * 2, CH, PB), F32),
            pltpu.VMEM((nq, NY * nz * 2, CH, PB), F32),
            pltpu.VMEM((nt, nj * local, 2 * PB), BF16),
            pltpu.VMEM((bands, nt, tri // bands, PB), F32),
            pltpu.VMEM((bands, nt, tri // bands, PB), F32),
            pltpu.VMEM((NY, 8, PB), jnp.int32),
            pltpu.SMEM((NY, 8, PB), jnp.int32),
            pltpu.SMEM((nt * nj,), jnp.int32),
            dma((3,)),
            dma((nq,)),
            dma((nq,)),
            dma((nq, nx)),
            dma((nq, nx)),
            dma((2,)),
            dma((2, nz // 2 + 1, nq)),
            dma((NY,)),
            dma((NY,)),
            dma,
            dma,
            dma((nq,)),
            dma((bands,)),
            dma((bands,)),
        ],
        compiler_params=pltpu.CompilerParams(
            collective_id=0, has_side_effects=True, vmem_limit_bytes=56 * 1024 * 1024
        ),
        cost_estimate=pl.CostEstimate(flops=1 << 30, bytes_accessed=4 << 20, transcendentals=0),
    )(bessel_table, spectrum, weights, need_owner, need_block)


def solution(mesh):
    return jax.shard_map(
        shards,
        mesh=mesh,
        in_specs=(
            P("band", "pair"),
            P("band", None),
            P("pair", None, None, "band"),
            P("pair", None),
            P("pair", None),
        ),
        out_specs=P("pair", "band", None),
        check_vma=False,
    )
```

```python
import functools

import jax
import jax.numpy as jnp
from jax import lax
from jax.experimental import pallas as pl
from jax.experimental.pallas import tpu as pltpu
from jax.sharding import PartitionSpec as P

PB = 128
NY = 4
CH = 8
UNIT = 16
GROUP = 4
LAG = 3
PACE = 2
MESH = pl.DeviceIdType.MESH
F32 = jnp.float32
BF16 = jnp.bfloat16


def z_order(nz, nq):
    half = nz // 2
    ready = [{(0, c): PACE * c for c in range(nq)} for _ in range(2)]
    ends = [{}, {}]
    order, time = [], 0
    while any(ready) or any(ends):
        slot = []
        for way in range(2):
            now = [k for k, at in ready[way].items() if at <= time]
            if now:
                d, c = min(now, key=lambda k: (k[1] // GROUP, k[0], k[1]))
                del ready[way][d, c]
                slot.append(("send", way, d, c))
                goes_on = d + 1 < half - 1 or (d + 1 == half - 1 and c % 2 == way)
                (ready if goes_on else ends)[way][d + 1, c] = time + LAG
            for d, c in sorted(k for k, at in ends[way].items() if at <= time):
                del ends[way][d, c]
                slot.append(("end", way, d, c))
        order.append(slot)
        time += 1
    return order


def kernel(
    sizes,
    table_in, spec_in, weights_in, owner_in, block_in,
    out,
    table, spec, weights, table_t, weights_t,
    part, core_in, band_in, ring, desk, picked, slots_0, slots_1, blocks, early,
    share, share_core, share_x,
    wants, wants_s, place_s,
    load_sem, core_send, core_recv, x_send, x_recv, z_send, z_recv,
    want_send, want_recv, want_local, y_send, y_recv,
    fc_send, fc_recv, fx_send, fx_recv,
):
    nx, nz, nq, nb, nt, nj, tri = sizes
    bands = 2 * nx
    units = nq * CH // UNIT
    per_unit = UNIT // CH
    groups = nq // GROUP
    slots = (slots_0, slots_1)
    pair = lax.axis_index("pair")
    band = lax.axis_index("band")
    z, y = pair // NY, lax.rem(pair, NY)
    x, core = band // 2, lax.rem(band, 2)
    rows = tri // bands

    def x_peer(i):
        return (pair, lax.rem(x + i, nx) * 2 + core)

    def y_peer(i):
        return (z * NY + lax.rem(y + i, NY), band)

    sibling = (pair, x * 2 + 1 - core)
    up = (lax.rem(z + 1, nz) * NY + y, band)
    down = (lax.rem(z + nz - 1, nz) * NY + y, band)

    barrier = pltpu.get_barrier_semaphore()
    partners = [x_peer(i) for i in range(1, nx)] + [y_peer(i) for i in range(1, NY)] + [up, down, sibling]
    for partner in partners:
        pl.semaphore_signal(barrier, inc=1, device_id=partner, device_id_type=MESH)

    loads = [
        pltpu.make_async_copy(src, dst, load_sem.at[i])
        for i, (src, dst) in enumerate(((table_in, table), (spec_in, spec), (weights_in, weights)))
    ]
    for load in loads:
        load.start()

    lane = lax.broadcasted_iota(jnp.int32, (8, PB), 1)
    row = lax.broadcasted_iota(jnp.int32, (8, PB), 0)
    zero = jnp.zeros((8, PB), jnp.int32)

    def want_row(t, carry):
        first, second, count = carry
        for j in range(nj):
            hit = lane == owner_in[t, j]
            number = block_in[t, j]
            first = jnp.where(hit & (count == 0), number, first)
            second = jnp.where(hit & (count == 1), number, second)
            count = count + hit.astype(jnp.int32)
        return first, second, count

    first, second, _ = lax.fori_loop(0, nt, want_row, (zero, zero, zero))
    wants[0] = jnp.where(row == 0, first, jnp.where(row == 1, second, 0))

    loads[0].wait()
    turned = table[...].T
    for b in range(bands):
        for u in range(units):
            at = (b * units + u) * UNIT
            table_t[u, b % 2, b // 2] = turned[at : at + UNIT]
    loads[1].wait()

    def hankel(u):
        left = table_t[u].reshape(bands * UNIT, table_t.shape[-1])
        product = jnp.dot(left, spec[...], preferred_element_type=F32)
        part[u] = product.reshape(2, nx, UNIT, nb * PB)

    def core_copy(u):
        return pltpu.make_async_remote_copy(
            part.at[u, 1 - core], core_in.at[u], core_send.at[u], core_recv.at[u],
            device_id=sibling, device_id_type=MESH,
        )

    def x_copy(c, i):
        some = pl.ds(c % per_unit * CH, CH)
        return pltpu.make_async_remote_copy(
            part.at[c // per_unit, core, lax.rem(x + i, nx), some], band_in.at[c, nx - i],
            x_send.at[c, i], x_recv.at[c, nx - i],
            device_id=x_peer(i), device_id_type=MESH,
        )

    def across_cores(u):
        core_copy(u).wait_recv()
        part[u, core] = part[u, core] + core_in[u]
        for c in range(u * per_unit, (u + 1) * per_unit):
            for i in range(1, nx):
                x_copy(c, i).start()

    def own_rows(c):
        for i in range(1, nx):
            pltpu.make_async_copy(band_in.at[c, i], band_in.at[c, i], x_recv.at[c, i]).wait()
        at = c % per_unit * CH
        total = part[c // per_unit, core, x, at : at + CH]
        for i in range(1, nx):
            total = total + band_in[c, i]
        for b in range(nb):
            ring[0, c, b] = total[:, b * PB : (b + 1) * PB]

    def want_copy(i):
        return pltpu.make_async_remote_copy(
            wants.at[0], wants.at[NY - i], want_send.at[i], want_recv.at[NY - i],
            device_id=y_peer(i), device_id_type=MESH,
        )

    hankel(0)
    pl.semaphore_wait(barrier, len(partners))
    core_copy(0).start()
    for i in range(1, NY):
        want_copy(i).start()
    for u in range(1, units):
        hankel(u)
        core_copy(u).start()
        across_cores(u - 1)
    across_cores(units - 1)

    to_scalar = pltpu.make_async_copy(wants, wants_s, want_local)
    for i in range(1, NY):
        pltpu.make_async_copy(wants.at[i], wants.at[i], want_recv.at[i]).wait()
    to_scalar.start()

    def place_row(t, carry):
        for j in range(nj):
            who = owner_in[t, j]
            rank = jnp.int32(0)
            for u in range(nt - 1):
                for k in range(nj):
                    same = (owner_in[u, k] == who) & (u < t)
                    rank = rank + same.astype(jnp.int32)
            dz = lax.rem(z - who // NY + nz, nz)
            dy = lax.rem(lax.rem(who, NY) - y + NY, NY)
            place_s[t * nj + j] = (dy * nz + dz) * 2 + jnp.minimum(rank, 1)
        return carry

    def turn(t, carry):
        for g in range(groups):
            at = g * GROUP * CH
            some = weights[t, :, at : at + GROUP * CH, :]
            weights_t[g, t] = some.reshape(nj * GROUP * CH, tri).T
        return carry

    def z_copy(way, d, c):
        here = d if way == 0 else (nz - d) % nz
        there = d + 1 if way == 0 else nz - d - 1
        return pltpu.make_async_remote_copy(
            ring.at[here, c], ring.at[there, c], z_send.at[way], z_recv.at[way, d + 1, c],
            device_id=up if way == 0 else down, device_id_type=MESH,
        )

    def z_wait(way, d, c):
        here = d if way == 0 else nz - d
        pltpu.make_async_copy(ring.at[here, c], ring.at[here, c], z_recv.at[way, d, c]).wait()

    def y_copy(i, g, here):
        return pltpu.make_async_remote_copy(
            picked.at[g, i, pl.ds(here * 2, 2)], slots[g].at[pl.ds(((NY - i) * nz + here) * 2, 2)],
            y_send, y_recv.at[g],
            device_id=y_peer(i), device_id_type=MESH,
        )

    done = {}

    def pick(here, c):
        g = c // GROUP
        at = c % GROUP * CH
        n = len(done) % 2
        done[here, c] = True
        desk[n] = ring[here, c]
        who = lax.rem(z + nz - here, nz) * NY + y
        for i in range(NY):
            for s in range(2):
                rows_of = desk[n, wants_s[i, s, who]]
                if i == 0:
                    slots[g][here * 2 + s, at : at + CH] = rows_of
                else:
                    picked[g, i, here * 2 + s, at : at + CH] = rows_of
        if all((here, k) in done for k in range(g * GROUP, (g + 1) * GROUP)):
            for i in range(1, NY):
                y_copy(i, g, here).start()

    def product(g, t):
        for j in range(nj):
            value = slots[g][place_s[t * nj + j]]
            high = value.astype(BF16)
            low = (value - high.astype(F32)).astype(BF16)
            at = j * GROUP * CH
            blocks[g, t, at : at + GROUP * CH, :PB] = high
            blocks[g, t, at : at + GROUP * CH, PB:] = low
        both = jnp.dot(weights_t[g, t], blocks[g, t], preferred_element_type=F32)
        return both[:, :PB] + both[:, PB:]

    def y_wait(g):
        whole = slots[g].at[pl.ds(nz * 2, (NY - 1) * nz * 2)]
        pltpu.make_async_copy(whole, whole, y_recv.at[g]).wait()

    def early_tile(g, t):
        total = product(g, t)
        early[t] = total if g == 0 else early[t] + total

    def early_group(g):
        y_wait(g)

        def body(t, carry):
            early_tile(g, t)
            return carry

        lax.fori_loop(0, nt, body, 0)

    order = z_order(nz, nq)
    last_of, own = {}, {}
    for n, slot in enumerate(order):
        for kind, way, d, c in slot:
            last_of[c // GROUP] = n
    lay_by = {min(last_of[g] + 8, len(order) - 1): g for g in range(groups - 1)}
    for n, slot in enumerate(order):
        for kind, way, d, c in slot:
            if d:
                z_wait(way, d, c)
            elif c not in own:
                own_rows(c)
                own[c] = n
            if kind == "send":
                z_copy(way, d, c).start()
        if n == 0:
            lax.fori_loop(0, nt, place_row, 0)
            loads[2].wait()
            lax.fori_loop(0, nt, turn, 0)
            to_scalar.wait()
        for kind, way, d, c in slot:
            if (d if way == 0 else (nz - d) % nz, c) not in done:
                pick(d if way == 0 else (nz - d) % nz, c)
        if n in lay_by:
            early_group(lay_by[n])

    def fc_copy(t):
        return pltpu.make_async_remote_copy(
            share.at[t, 1 - core], share_core.at[t], fc_send.at[t], fc_recv.at[t],
            device_id=sibling, device_id_type=MESH,
        )

    def fx_copy(t, i):
        return pltpu.make_async_remote_copy(
            share.at[t, core, lax.rem(x + i, nx)], share_x.at[t, nx - i],
            fx_send.at[t, i], fx_recv.at[t, nx - i],
            device_id=x_peer(i), device_id_type=MESH,
        )

    y_wait(groups - 1)

    def last_tile(t, carry):
        total = product(groups - 1, t)
        if groups > 1:
            total = total + early[t]
        for b in range(bands):
            share[t, b % 2, b // 2] = total[b * rows : (b + 1) * rows]
        fc_copy(t).start()
        return carry

    lax.fori_loop(0, nt, last_tile, 0)
    for t in range(nt):
        fc_copy(t).wait_recv()
        share[t, core] = share[t, core] + share_core[t]
        for i in range(1, nx):
            fx_copy(t, i).start()
    for t in range(nt):
        total = share[t, core, x]
        for i in range(1, nx):
            pltpu.make_async_copy(share_x.at[t, i], share_x.at[t, i], fx_recv.at[t, i]).wait()
            total = total + share_x[t, i]
        out[t] = total

    for u in range(units):
        core_copy(u).wait_send()
    for c in range(nq):
        for i in range(1, nx):
            x_copy(c, i).wait_send()
    for i in range(1, NY):
        want_copy(i).wait_send()
    for t in range(nt):
        fc_copy(t).wait_send()
        for i in range(1, nx):
            fx_copy(t, i).wait_send()
    for way in range(2):
        sent = sum(kind == "send" and w == way for slot in order for kind, w, _, _ in slot)
        whole = ring.at[pl.ds(0, sent // nq)]
        pltpu.make_async_copy(whole, whole, z_send.at[way]).wait()
        if sent % nq:
            some = ring.at[0, pl.ds(0, sent % nq)]
            pltpu.make_async_copy(some, some, z_send.at[way]).wait()
    whole = picked.at[:, pl.ds(1, NY - 1)]
    pltpu.make_async_copy(whole, whole, y_send).wait()


def shards(spectrum, bessel_table, interp_weights, need_owner, need_block):
    bands = lax.axis_size("band")
    nz = lax.axis_size("pair") // NY
    nx = bands // 2
    depth, radial = bessel_table.shape
    nb = spectrum.shape[1] // PB
    nt, nj, tri, local = interp_weights.shape
    nq = local // CH
    units = local // UNIT
    groups = nq // GROUP
    wide = GROUP * CH
    rows = tri // bands
    sizes = (nx, nz, nq, nb, nt, nj, tri)
    weights = jnp.swapaxes(interp_weights, 2, 3)
    dma = pltpu.SemaphoreType.DMA
    return pl.pallas_call(
        functools.partial(kernel, sizes),
        out_shape=jax.ShapeDtypeStruct((nt, rows, PB), F32),
        in_specs=[pl.BlockSpec(memory_space=pl.ANY)] * 3
        + [pl.BlockSpec(memory_space=pltpu.SMEM)] * 2,
        out_specs=pl.BlockSpec(memory_space=pltpu.VMEM),
        scratch_shapes=[
            pltpu.VMEM((depth, radial), BF16),
            pltpu.VMEM(spectrum.shape, BF16),
            pltpu.VMEM(weights.shape, BF16),
            pltpu.VMEM((units, 2, nx, UNIT, depth), BF16),
            pltpu.VMEM((groups, nt, tri, nj * wide), BF16),
            pltpu.VMEM((units, 2, nx, UNIT, nb * PB), F32),
            pltpu.VMEM((units, nx, UNIT, nb * PB), F32),
            pltpu.VMEM((nq, nx, CH, nb * PB), F32),
            pltpu.VMEM((nz, nq, nb, CH, PB), F32),
            pltpu.VMEM((2, nb, CH, PB), F32),
            pltpu.VMEM((groups, NY, nz * 2, wide, PB), F32),
            pltpu.VMEM((NY * nz * 2, wide, PB), F32),
            pltpu.VMEM((NY * nz * 2, wide, PB), F32),
            pltpu.VMEM((groups, nt, nj * wide, 2 * PB), BF16),
            pltpu.VMEM((nt, tri, PB), F32),
            pltpu.VMEM((nt, 2, nx, rows, PB), F32),
            pltpu.VMEM((nt, nx, rows, PB), F32),
            pltpu.VMEM((nt, nx, rows, PB), F32),
            pltpu.VMEM((NY, 8, PB), jnp.int32),
            pltpu.SMEM((NY, 8, PB), jnp.int32),
            pltpu.SMEM((nt * nj,), jnp.int32),
            dma((3,)),
            dma((units,)),
            dma((units,)),
            dma((nq, nx)),
            dma((nq, nx)),
            dma((2,)),
            dma((2, nz // 2 + 1, nq)),
            dma((NY,)),
            dma((NY,)),
            dma,
            dma,
            dma((groups,)),
            dma((nt,)),
            dma((nt,)),
            dma((nt, nx)),
            dma((nt, nx)),
        ],
        compiler_params=pltpu.CompilerParams(
            collective_id=0, has_side_effects=True, vmem_limit_bytes=56 * 1024 * 1024
        ),
        cost_estimate=pl.CostEstimate(flops=1 << 30, bytes_accessed=4 << 20, transcendentals=0),
    )(bessel_table, spectrum, weights, need_owner, need_block)


def solution(mesh):
    return jax.shard_map(
        shards,
        mesh=mesh,
        in_specs=(
            P("band", "pair"),
            P("band", None),
            P("pair", None, None, "band"),
            P("pair", None),
            P("pair", None),
        ),
        out_specs=P("pair", "band", None),
        check_vma=False,
    )
```

```python
import functools

import jax
import jax.numpy as jnp
from jax import lax
from jax.experimental import pallas as pl
from jax.experimental.pallas import tpu as pltpu
from jax.sharding import PartitionSpec as P

PB = 128
NY = 4
CH = 8
UNIT = 16
GROUP = 4
LAG = 4
LATE = 3
PACE = 2
AHEAD = 3
MESH = pl.DeviceIdType.MESH
F32 = jnp.float32
BF16 = jnp.bfloat16


def z_order(nz, nq):
    half = nz // 2
    ready = [{(0, c): PACE * c for c in range(nq)} for _ in range(2)]
    ends = [{}, {}]
    order, time = [], 0
    while any(ready) or any(ends):
        slot = []
        for way in range(2):
            now = [k for k, at in ready[way].items() if at <= time]
            if now:
                d, c = min(now, key=lambda k: (k[1] // GROUP, k[0], k[1]))
                del ready[way][d, c]
                slot.append(("send", way, d, c))
                goes_on = d + 1 < half - 1 or (d + 1 == half - 1 and c % 2 == way)
                (ready if goes_on else ends)[way][d + 1, c] = time + LAG
            for d, c in sorted(k for k, at in ends[way].items() if at <= time):
                del ends[way][d, c]
                slot.append(("end", way, d, c))
        order.append(slot)
        time += 1
    return order


def kernel(
    sizes,
    table_in, spec_in, weights_in, owner_hbm, block_hbm,
    out,
    owner_in, block_in,
    table, spec, weights, table_t, weights_t,
    part, core_in, band_in, ring, desk, picked, slots_0, slots_1, blocks, early,
    share, share_core, share_x,
    wants, wants_s, place_s,
    load_sem, core_send, core_recv, x_send, x_recv, z_send, z_recv,
    want_send, want_recv, want_local, y_send, y_recv,
    fc_send, fc_recv, fx_send, fx_recv,
):
    nx, nz, nq, nb, nt, nj, tri = sizes
    bands = 2 * nx
    units = nq * CH // UNIT
    per_unit = UNIT // CH
    groups = nq // GROUP
    slots = (slots_0, slots_1)
    pair = lax.axis_index("pair")
    band = lax.axis_index("band")
    z, y = pair // NY, lax.rem(pair, NY)
    x, core = band // 2, lax.rem(band, 2)
    rows = tri // bands
    x_order = sorted(range(1, nx), key=lambda i: -min(i, nx - i))

    def x_peer(i):
        return (pair, lax.rem(x + i, nx) * 2 + core)

    def y_peer(i):
        return (z * NY + lax.rem(y + i, NY), band)

    sibling = (pair, x * 2 + 1 - core)
    up = (lax.rem(z + 1, nz) * NY + y, band)
    down = (lax.rem(z + nz - 1, nz) * NY + y, band)

    loads = [
        pltpu.make_async_copy(src, dst, load_sem.at[i])
        for i, (src, dst) in enumerate((
            (table_in, table), (spec_in, spec), (weights_in, weights),
            (owner_hbm, owner_in), (block_hbm, block_in),
        ))
    ]
    for i in (0, 1, 3, 4, 2):
        loads[i].start()

    barrier = pltpu.get_barrier_semaphore()
    partners = [x_peer(i) for i in range(1, nx)] + [y_peer(i) for i in range(1, NY)] + [up, down, sibling]
    for partner in partners:
        pl.semaphore_signal(barrier, inc=1, device_id=partner, device_id_type=MESH)

    loads[3].wait()
    loads[4].wait()
    lane = lax.broadcasted_iota(jnp.int32, (8, PB), 1)
    row = lax.broadcasted_iota(jnp.int32, (8, PB), 0)
    zero = jnp.zeros((8, PB), jnp.int32)

    def want_row(t, carry):
        first, second, count = carry
        for j in range(nj):
            hit = lane == owner_in[t, j]
            number = block_in[t, j]
            first = jnp.where(hit & (count == 0), number, first)
            second = jnp.where(hit & (count == 1), number, second)
            count = count + hit.astype(jnp.int32)
        return first, second, count

    first, second, _ = lax.fori_loop(0, nt, want_row, (zero, zero, zero))
    wants[0] = jnp.where(row == 0, first, jnp.where(row == 1, second, 0))

    loads[0].wait()
    turned = table[...].T
    for b in range(bands):
        for u in range(units):
            at = (b * units + u) * UNIT
            table_t[u, b % 2, b // 2] = turned[at : at + UNIT]
    loads[1].wait()

    def hankel(u):
        left = table_t[u].reshape(bands * UNIT, table_t.shape[-1])
        product = jnp.dot(left, spec[...], preferred_element_type=F32)
        part[u] = product.reshape(2, nx, UNIT, nb * PB)

    def core_copy(u):
        return pltpu.make_async_remote_copy(
            part.at[u, 1 - core], core_in.at[u], core_send.at[u], core_recv.at[u],
            device_id=sibling, device_id_type=MESH,
        )

    def x_copy(c, i):
        some = pl.ds(c % per_unit * CH, CH)
        return pltpu.make_async_remote_copy(
            part.at[c // per_unit, core, lax.rem(x + i, nx), some], band_in.at[c, nx - i],
            x_send.at[c, i], x_recv.at[c, nx - i],
            device_id=x_peer(i), device_id_type=MESH,
        )

    def x_start(c):
        for i in x_order:
            x_copy(c, i).start()

    def across_cores(u):
        core_copy(u).wait_recv()
        part[u, core] = part[u, core] + core_in[u]
        for c in range(u * per_unit, (u + 1) * per_unit):
            if c < AHEAD:
                x_start(c)

    def own_rows(c):
        for i in range(1, nx):
            pltpu.make_async_copy(band_in.at[c, i], band_in.at[c, i], x_recv.at[c, i]).wait()
        at = c % per_unit * CH
        total = part[c // per_unit, core, x, at : at + CH]
        for i in range(1, nx):
            total = total + band_in[c, i]
        for b in range(nb):
            ring[0, c, b] = total[:, b * PB : (b + 1) * PB]
        if c + AHEAD < nq:
            x_start(c + AHEAD)

    def want_copy(i):
        return pltpu.make_async_remote_copy(
            wants.at[0], wants.at[NY - i], want_send.at[i], want_recv.at[NY - i],
            device_id=y_peer(i), device_id_type=MESH,
        )

    hankel(0)
    pl.semaphore_wait(barrier, len(partners))
    core_copy(0).start()
    for i in range(1, NY):
        want_copy(i).start()
    for u in range(1, units):
        hankel(u)
        core_copy(u).start()
        across_cores(u - 1)
    across_cores(units - 1)

    to_scalar = pltpu.make_async_copy(wants, wants_s, want_local)
    for i in range(1, NY):
        pltpu.make_async_copy(wants.at[i], wants.at[i], want_recv.at[i]).wait()
    to_scalar.start()

    def place_row(t):
        for j in range(nj):
            who = owner_in[t, j]
            rank = jnp.int32(0)
            for u in range(t):
                for k in range(nj):
                    rank = rank + (owner_in[u, k] == who).astype(jnp.int32)
            dz = lax.rem(z - who // NY + nz, nz)
            dy = lax.rem(lax.rem(who, NY) - y + NY, NY)
            place_s[t * nj + j] = (dy * nz + dz) * 2 + jnp.minimum(rank, 1)

    def turn(t):
        for g in range(groups):
            at = g * GROUP * CH
            some = weights[t, :, at : at + GROUP * CH, :]
            weights_t[g, t] = some.reshape(nj * GROUP * CH, tri).T

    def z_copy(way, d, c):
        here = d if way == 0 else (nz - d) % nz
        there = d + 1 if way == 0 else nz - d - 1
        return pltpu.make_async_remote_copy(
            ring.at[here, c], ring.at[there, c], z_send.at[way], z_recv.at[way, d + 1, c],
            device_id=up if way == 0 else down, device_id_type=MESH,
        )

    def z_wait(way, d, c):
        here = d if way == 0 else nz - d
        pltpu.make_async_copy(ring.at[here, c], ring.at[here, c], z_recv.at[way, d, c]).wait()

    def y_copy(i, g, here, at, count):
        some = pl.ds(at, count)
        return pltpu.make_async_remote_copy(
            picked.at[g, i, pl.ds(here * 2, 2), some],
            slots[g].at[pl.ds(((NY - i) * nz + here) * 2, 2), some],
            y_send, y_recv.at[g],
            device_id=y_peer(i), device_id_type=MESH,
        )

    done = {}

    def pick(here, c):
        g = c // GROUP
        at = c % GROUP * CH
        n = len(done) % 2
        done[here, c] = True
        desk[n] = ring[here, c]
        who = lax.rem(z + nz - here, nz) * NY + y
        for i in range(NY):
            for s in range(2):
                rows_of = desk[n, wants_s[i, s, who]]
                if i == 0:
                    slots[g][here * 2 + s, at : at + CH] = rows_of
                else:
                    picked[g, i, here * 2 + s, at : at + CH] = rows_of
        if g == groups - 1 and abs(here - nz // 2) <= LATE:
            for i in range(1, NY):
                y_copy(i, g, here, at, CH).start()
        elif all((here, k) in done for k in range(g * GROUP, (g + 1) * GROUP)):
            for i in range(1, NY):
                y_copy(i, g, here, 0, GROUP * CH).start()

    def product(g, t):
        for j in range(nj):
            value = slots[g][place_s[t * nj + j]]
            high = value.astype(BF16)
            low = (value - high.astype(F32)).astype(BF16)
            at = j * GROUP * CH
            blocks[g, t, at : at + GROUP * CH, :PB] = high
            blocks[g, t, at : at + GROUP * CH, PB:] = low
        both = jnp.dot(weights_t[g, t], blocks[g, t], preferred_element_type=F32)
        return both[:, :PB] + both[:, PB:]

    def y_wait(g):
        whole = slots[g].at[pl.ds(nz * 2, (NY - 1) * nz * 2)]
        pltpu.make_async_copy(whole, whole, y_recv.at[g]).wait()

    def early_tile(g, t):
        total = product(g, t)
        early[t] = total if g == 0 else early[t] + total

    order = z_order(nz, nq)
    last_of, own = {}, {}
    for n, slot in enumerate(order):
        for kind, way, d, c in slot:
            last_of[c // GROUP] = n
    lay_by = {min(last_of[g] + 8 + 2 * t, len(order) - 1 - nt + t): (g, t) for g in range(groups - 1) for t in range(nt)}
    set_up = {min(12 + 2 * t, len(order) - 1 - nt + t): t for t in range(nt)}
    for n, slot in enumerate(order):
        for kind, way, d, c in slot:
            if d:
                z_wait(way, d, c)
            elif c not in own:
                own_rows(c)
                own[c] = n
            if kind == "send":
                z_copy(way, d, c).start()
        if n == 0:
            to_scalar.wait()
        for kind, way, d, c in slot:
            if (d if way == 0 else (nz - d) % nz, c) not in done:
                pick(d if way == 0 else (nz - d) % nz, c)
        if n in set_up:
            place_row(set_up[n])
            if set_up[n] == 0:
                loads[2].wait()
            turn(set_up[n])
        if n in lay_by:
            g, t = lay_by[n]
            if t == 0:
                y_wait(g)
            early_tile(g, t)

    def fc_copy(t):
        return pltpu.make_async_remote_copy(
            share.at[t, 1 - core], share_core.at[t], fc_send.at[t], fc_recv.at[t],
            device_id=sibling, device_id_type=MESH,
        )

    def fx_copy(t, i):
        return pltpu.make_async_remote_copy(
            share.at[t, core, lax.rem(x + i, nx)], share_x.at[t, nx - i],
            fx_send.at[t, i], fx_recv.at[t, nx - i],
            device_id=x_peer(i), device_id_type=MESH,
        )

    y_wait(groups - 1)

    for t in range(nt):
        total = product(groups - 1, t)
        if groups > 1:
            total = total + early[t]
        for b in range(bands):
            share[t, b % 2, b // 2] = total[b * rows : (b + 1) * rows]
        fc_copy(t).start()
    for t in range(nt):
        fc_copy(t).wait_recv()
        share[t, core] = share[t, core] + share_core[t]
        for i in x_order:
            fx_copy(t, i).start()
    for u in range(units):
        core_copy(u).wait_send()
    for c in range(nq):
        for i in range(1, nx):
            x_copy(c, i).wait_send()
    for i in range(1, NY):
        want_copy(i).wait_send()
    for way in range(2):
        sent = sum(kind == "send" and w == way for slot in order for kind, w, _, _ in slot)
        whole = ring.at[pl.ds(0, sent // nq)]
        pltpu.make_async_copy(whole, whole, z_send.at[way]).wait()
        if sent % nq:
            some = ring.at[0, pl.ds(0, sent % nq)]
            pltpu.make_async_copy(some, some, z_send.at[way]).wait()
    whole = picked.at[:, pl.ds(1, NY - 1)]
    pltpu.make_async_copy(whole, whole, y_send).wait()

    for t in range(nt):
        total = share[t, core, x]
        for i in range(1, nx):
            pltpu.make_async_copy(share_x.at[t, i], share_x.at[t, i], fx_recv.at[t, i]).wait()
            total = total + share_x[t, i]
        out[t] = total

    for t in range(nt):
        fc_copy(t).wait_send()
        for i in range(1, nx):
            fx_copy(t, i).wait_send()


def shards(spectrum, bessel_table, interp_weights, need_owner, need_block):
    bands = lax.axis_size("band")
    nz = lax.axis_size("pair") // NY
    nx = bands // 2
    depth, radial = bessel_table.shape
    nb = spectrum.shape[1] // PB
    nt, nj, tri, local = interp_weights.shape
    nq = local // CH
    units = local // UNIT
    groups = nq // GROUP
    wide = GROUP * CH
    rows = tri // bands
    sizes = (nx, nz, nq, nb, nt, nj, tri)
    weights = jnp.swapaxes(interp_weights, 2, 3)
    dma = pltpu.SemaphoreType.DMA
    return pl.pallas_call(
        functools.partial(kernel, sizes),
        out_shape=jax.ShapeDtypeStruct((nt, rows, PB), F32),
        in_specs=[pl.BlockSpec(memory_space=pl.ANY)] * 5,
        out_specs=pl.BlockSpec(memory_space=pltpu.VMEM),
        scratch_shapes=[
            pltpu.SMEM(need_owner.shape, jnp.int32),
            pltpu.SMEM(need_block.shape, jnp.int32),
            pltpu.VMEM((depth, radial), BF16),
            pltpu.VMEM(spectrum.shape, BF16),
            pltpu.VMEM(weights.shape, BF16),
            pltpu.VMEM((units, 2, nx, UNIT, depth), BF16),
            pltpu.VMEM((groups, nt, tri, nj * wide), BF16),
            pltpu.VMEM((units, 2, nx, UNIT, nb * PB), F32),
            pltpu.VMEM((units, nx, UNIT, nb * PB), F32),
            pltpu.VMEM((nq, nx, CH, nb * PB), F32),
            pltpu.VMEM((nz, nq, nb, CH, PB), F32),
            pltpu.VMEM((2, nb, CH, PB), F32),
            pltpu.VMEM((groups, NY, nz * 2, wide, PB), F32),
            pltpu.VMEM((NY * nz * 2, wide, PB), F32),
            pltpu.VMEM((NY * nz * 2, wide, PB), F32),
            pltpu.VMEM((groups, nt, nj * wide, 2 * PB), BF16),
            pltpu.VMEM((nt, tri, PB), F32),
            pltpu.VMEM((nt, 2, nx, rows, PB), F32),
            pltpu.VMEM((nt, nx, rows, PB), F32),
            pltpu.VMEM((nt, nx, rows, PB), F32),
            pltpu.VMEM((NY, 8, PB), jnp.int32),
            pltpu.SMEM((NY, 8, PB), jnp.int32),
            pltpu.SMEM((nt * nj,), jnp.int32),
            dma((5,)),
            dma((units,)),
            dma((units,)),
            dma((nq, nx)),
            dma((nq, nx)),
            dma((2,)),
            dma((2, nz // 2 + 1, nq)),
            dma((NY,)),
            dma((NY,)),
            dma,
            dma,
            dma((groups,)),
            dma((nt,)),
            dma((nt,)),
            dma((nt, nx)),
            dma((nt, nx)),
        ],
        compiler_params=pltpu.CompilerParams(
            collective_id=0, has_side_effects=True, vmem_limit_bytes=56 * 1024 * 1024
        ),
        cost_estimate=pl.CostEstimate(flops=1 << 30, bytes_accessed=4 << 20, transcendentals=0),
    )(bessel_table, spectrum, weights, need_owner, need_block)


def solution(mesh):
    return jax.shard_map(
        shards,
        mesh=mesh,
        in_specs=(
            P("band", "pair"),
            P("band", None),
            P("pair", None, None, "band"),
            P("pair", None),
            P("pair", None),
        ),
        out_specs=P("pair", "band", None),
        check_vma=False,
    )
```

```python
import functools

import jax
import jax.numpy as jnp
from jax import lax
from jax.experimental import pallas as pl
from jax.experimental.pallas import tpu as pltpu
from jax.sharding import PartitionSpec as P

PB = 128
NY = 4
CH = 8
UNIT = 16
GROUP = 4
LAG = 4
LATE = 3
PACE = 2
AHEAD = 3
MESH = pl.DeviceIdType.MESH
F32 = jnp.float32
BF16 = jnp.bfloat16


def z_order(nz, nq):
    half = nz // 2
    ready = [{(0, c): PACE * c for c in range(nq)} for _ in range(2)]
    ends = [{}, {}]
    order, time = [], 0
    while any(ready) or any(ends):
        slot = []
        for way in range(2):
            now = [k for k, at in ready[way].items() if at <= time]
            if now:
                d, c = min(now, key=lambda k: (k[1] // GROUP, k[0], k[1]))
                del ready[way][d, c]
                slot.append(("send", way, d, c))
                goes_on = d + 1 < half - 1 or (d + 1 == half - 1 and c % 2 == way)
                (ready if goes_on else ends)[way][d + 1, c] = time + LAG
            for d, c in sorted(k for k, at in ends[way].items() if at <= time):
                del ends[way][d, c]
                slot.append(("end", way, d, c))
        order.append(slot)
        time += 1
    return order


def kernel(
    sizes,
    table_in, spec_in, weights_in, owner_hbm, block_hbm,
    out,
    owner_in, block_in,
    table, spec, weights, table_t, weights_t,
    part, core_in, band_in, ring, desk, picked, slots_0, slots_1, blocks, early,
    share, share_core, share_x,
    wants, wants_s, place_s, far_wants, far_s, far_out, far_in,
    load_sem, core_send, core_recv, x_send, x_recv, z_send, z_recv,
    want_send, want_recv, want_local, y_send, y_recv, fw_send, fw_recv, far_local, far_send,
    fc_send, fc_recv, fx_send, fx_recv,
):
    nx, nz, nq, nb, nt, nj, tri = sizes
    bands = 2 * nx
    half = nz // 2
    units = nq * CH // UNIT
    per_unit = UNIT // CH
    groups = nq // GROUP
    slots = (slots_0, slots_1)
    pair = lax.axis_index("pair")
    band = lax.axis_index("band")
    z, y = pair // NY, lax.rem(pair, NY)
    x, core = band // 2, lax.rem(band, 2)
    rows = tri // bands
    x_order = sorted(range(1, nx), key=lambda i: -min(i, nx - i))

    def x_peer(i):
        return (pair, lax.rem(x + i, nx) * 2 + core)

    def y_peer(i):
        return (z * NY + lax.rem(y + i, NY), band)

    sibling = (pair, x * 2 + 1 - core)
    up = (lax.rem(z + 1, nz) * NY + y, band)
    down = (lax.rem(z + nz - 1, nz) * NY + y, band)

    loads = [
        pltpu.make_async_copy(src, dst, load_sem.at[i])
        for i, (src, dst) in enumerate((
            (table_in, table), (spec_in, spec), (weights_in, weights),
            (owner_hbm, owner_in), (block_hbm, block_in),
        ))
    ]
    for i in (0, 1, 3, 4, 2):
        loads[i].start()

    barrier = pltpu.get_barrier_semaphore()
    partners = [x_peer(i) for i in range(1, nx)] + [y_peer(i) for i in range(1, NY)] + [up, down, sibling]
    for partner in partners:
        pl.semaphore_signal(barrier, inc=1, device_id=partner, device_id_type=MESH)

    loads[3].wait()
    loads[4].wait()
    lane = lax.broadcasted_iota(jnp.int32, (8, PB), 1)
    row = lax.broadcasted_iota(jnp.int32, (8, PB), 0)
    zero = jnp.zeros((8, PB), jnp.int32)

    def want_row(t, carry):
        first, second, count = carry
        for j in range(nj):
            hit = lane == owner_in[t, j]
            number = block_in[t, j]
            first = jnp.where(hit & (count == 0), number, first)
            second = jnp.where(hit & (count == 1), number, second)
            count = count + hit.astype(jnp.int32)
        return first, second, count

    first, second, _ = lax.fori_loop(0, nt, want_row, (zero, zero, zero))
    wants[0] = jnp.where(row == 0, first, jnp.where(row == 1, second, 0))

    loads[0].wait()
    turned = table[...].T
    for b in range(bands):
        for u in range(units):
            at = (b * units + u) * UNIT
            table_t[u, b % 2, b // 2] = turned[at : at + UNIT]
    loads[1].wait()

    def hankel(u):
        left = table_t[u].reshape(bands * UNIT, table_t.shape[-1])
        product = jnp.dot(left, spec[...], preferred_element_type=F32)
        part[u] = product.reshape(2, nx, UNIT, nb * PB)

    def core_copy(u):
        return pltpu.make_async_remote_copy(
            part.at[u, 1 - core], core_in.at[u], core_send.at[u], core_recv.at[u],
            device_id=sibling, device_id_type=MESH,
        )

    def x_copy(c, i):
        some = pl.ds(c % per_unit * CH, CH)
        return pltpu.make_async_remote_copy(
            part.at[c // per_unit, core, lax.rem(x + i, nx), some], band_in.at[c, nx - i],
            x_send.at[c, i], x_recv.at[c, nx - i],
            device_id=x_peer(i), device_id_type=MESH,
        )

    def x_start(c):
        for i in x_order:
            x_copy(c, i).start()

    def across_cores(u):
        core_copy(u).wait_recv()
        part[u, core] = part[u, core] + core_in[u]
        for c in range(u * per_unit, (u + 1) * per_unit):
            if c < AHEAD:
                x_start(c)

    def own_rows(c):
        for i in range(1, nx):
            pltpu.make_async_copy(band_in.at[c, i], band_in.at[c, i], x_recv.at[c, i]).wait()
        at = c % per_unit * CH
        total = part[c // per_unit, core, x, at : at + CH]
        for i in range(1, nx):
            total = total + band_in[c, i]
        for b in range(nb):
            ring[0, c, b] = total[:, b * PB : (b + 1) * PB]
        if c + AHEAD < nq:
            x_start(c + AHEAD)

    def want_copy(i):
        return pltpu.make_async_remote_copy(
            wants.at[0], wants.at[NY - i], want_send.at[i], want_recv.at[NY - i],
            device_id=y_peer(i), device_id_type=MESH,
        )

    hankel(0)
    pl.semaphore_wait(barrier, len(partners))
    core_copy(0).start()
    for i in range(1, NY):
        want_copy(i).start()
    for u in range(1, units):
        hankel(u)
        core_copy(u).start()
        across_cores(u - 1)
    across_cores(units - 1)

    to_scalar = pltpu.make_async_copy(wants, wants_s, want_local)
    for i in range(1, NY):
        pltpu.make_async_copy(wants.at[i], wants.at[i], want_recv.at[i]).wait()
    to_scalar.start()

    def far_want_copy(way):
        return pltpu.make_async_remote_copy(
            wants, far_wants.at[1 - way], fw_send.at[way], fw_recv.at[1 - way],
            device_id=up if way == 0 else down, device_id_type=MESH,
        )

    for way in range(2):
        far_want_copy(way).start()
    to_far = pltpu.make_async_copy(far_wants, far_s, far_local)

    def place_row(t):
        for j in range(nj):
            who = owner_in[t, j]
            rank = jnp.int32(0)
            for u in range(t):
                for k in range(nj):
                    rank = rank + (owner_in[u, k] == who).astype(jnp.int32)
            dz = lax.rem(z - who // NY + nz, nz)
            dy = lax.rem(lax.rem(who, NY) - y + NY, NY)
            place_s[t * nj + j] = (dy * nz + dz) * 2 + jnp.minimum(rank, 1)

    def turn(t):
        for g in range(groups):
            at = g * GROUP * CH
            some = weights[t, :, at : at + GROUP * CH, :]
            weights_t[g, t] = some.reshape(nj * GROUP * CH, tri).T

    def z_copy(way, d, c):
        here = d if way == 0 else (nz - d) % nz
        there = d + 1 if way == 0 else nz - d - 1
        return pltpu.make_async_remote_copy(
            ring.at[here, c], ring.at[there, c], z_send.at[way], z_recv.at[way, d + 1, c],
            device_id=up if way == 0 else down, device_id_type=MESH,
        )

    def z_wait(way, d, c):
        here = d if way == 0 else nz - d
        what = far_in.at[c] if d == half else ring.at[here, c]
        pltpu.make_async_copy(what, what, z_recv.at[way, d, c]).wait()

    def far_copy(way, c):
        return pltpu.make_async_remote_copy(
            far_out.at[c], far_in.at[c], far_send, z_recv.at[way, half, c],
            device_id=up if way == 0 else down, device_id_type=MESH,
        )

    def far_go(way, c):
        here = half - 1 if way == 0 else nz - half + 1
        desk[2] = ring[here, c]
        who = lax.rem(z + nz - here, nz) * NY + y
        for i in range(NY):
            for s in range(2):
                far_out[c, i * 2 + s] = desk[2, far_s[way, i, s, who]]
        far_copy(way, c).start()

    def far_come(c):
        g = c // GROUP
        at = c % GROUP * CH
        done[half, c] = True
        slots[g][half * 2 : half * 2 + 2, at : at + CH] = far_in[c, 0:2]
        for i in range(1, NY):
            pltpu.make_async_remote_copy(
                far_in.at[c, pl.ds(i * 2, 2)],
                slots[g].at[pl.ds(((NY - i) * nz + half) * 2, 2), pl.ds(at, CH)],
                y_send, y_recv.at[g],
                device_id=y_peer(i), device_id_type=MESH,
            ).start()

    def y_copy(i, g, here, at, count):
        some = pl.ds(at, count)
        return pltpu.make_async_remote_copy(
            picked.at[g, i, pl.ds(here * 2, 2), some],
            slots[g].at[pl.ds(((NY - i) * nz + here) * 2, 2), some],
            y_send, y_recv.at[g],
            device_id=y_peer(i), device_id_type=MESH,
        )

    done = {}

    def pick(here, c):
        g = c // GROUP
        at = c % GROUP * CH
        n = len(done) % 2
        done[here, c] = True
        desk[n] = ring[here, c]
        who = lax.rem(z + nz - here, nz) * NY + y
        for i in range(NY):
            for s in range(2):
                rows_of = desk[n, wants_s[i, s, who]]
                if i == 0:
                    slots[g][here * 2 + s, at : at + CH] = rows_of
                else:
                    picked[g, i, here * 2 + s, at : at + CH] = rows_of
        if g == groups - 1 and abs(here - nz // 2) <= LATE:
            for i in range(1, NY):
                y_copy(i, g, here, at, CH).start()
        elif all((here, k) in done for k in range(g * GROUP, (g + 1) * GROUP)):
            for i in range(1, NY):
                y_copy(i, g, here, 0, GROUP * CH).start()

    def product(g, t):
        for j in range(nj):
            value = slots[g][place_s[t * nj + j]]
            high = value.astype(BF16)
            low = (value - high.astype(F32)).astype(BF16)
            at = j * GROUP * CH
            blocks[g, t, at : at + GROUP * CH, :PB] = high
            blocks[g, t, at : at + GROUP * CH, PB:] = low
        both = jnp.dot(weights_t[g, t], blocks[g, t], preferred_element_type=F32)
        return both[:, :PB] + both[:, PB:]

    def y_wait(g):
        whole = slots[g].at[pl.ds(nz * 2, (NY - 1) * nz * 2)]
        pltpu.make_async_copy(whole, whole, y_recv.at[g]).wait()

    def early_tile(g, t):
        total = product(g, t)
        early[t] = total if g == 0 else early[t] + total

    order = z_order(nz, nq)
    last_of, own, far_ready = {}, {}, []
    for n, slot in enumerate(order):
        for kind, way, d, c in slot:
            last_of[c // GROUP] = n
    lay_by = {min(last_of[g] + 8 + 2 * t, len(order) - 1 - nt + t): (g, t) for g in range(groups - 1) for t in range(nt)}
    set_up = {min(12 + 2 * t, len(order) - 1 - nt + t): t for t in range(nt)}
    for n, slot in enumerate(order):
        for kind, way, d, c in slot:
            if d:
                z_wait(way, d, c)
            elif c not in own:
                own_rows(c)
                own[c] = n
            if kind == "send" and d == half - 1:
                if not far_ready:
                    for w in range(2):
                        pltpu.make_async_copy(far_wants.at[w], far_wants.at[w], fw_recv.at[w]).wait()
                    to_far.start()
                    to_far.wait()
                    far_ready.append(n)
                far_go(way, c)
            elif kind == "send":
                z_copy(way, d, c).start()
        if n == 0:
            to_scalar.wait()
        for kind, way, d, c in slot:
            if d == half:
                far_come(c)
            elif (d if way == 0 else (nz - d) % nz, c) not in done:
                pick(d if way == 0 else (nz - d) % nz, c)
        if n in set_up:
            place_row(set_up[n])
            if set_up[n] == 0:
                loads[2].wait()
            turn(set_up[n])
        if n in lay_by:
            g, t = lay_by[n]
            if t == 0:
                y_wait(g)
            early_tile(g, t)

    def fc_copy(t):
        return pltpu.make_async_remote_copy(
            share.at[t, 1 - core], share_core.at[t], fc_send.at[t], fc_recv.at[t],
            device_id=sibling, device_id_type=MESH,
        )

    def fx_copy(t, i):
        return pltpu.make_async_remote_copy(
            share.at[t, core, lax.rem(x + i, nx)], share_x.at[t, nx - i],
            fx_send.at[t, i], fx_recv.at[t, nx - i],
            device_id=x_peer(i), device_id_type=MESH,
        )

    y_wait(groups - 1)

    for t in range(nt):
        total = product(groups - 1, t)
        if groups > 1:
            total = total + early[t]
        for b in range(bands):
            share[t, b % 2, b // 2] = total[b * rows : (b + 1) * rows]
        fc_copy(t).start()
    for t in range(nt):
        fc_copy(t).wait_recv()
        share[t, core] = share[t, core] + share_core[t]
        for i in x_order:
            fx_copy(t, i).start()
    for u in range(units):
        core_copy(u).wait_send()
    for c in range(nq):
        for i in range(1, nx):
            x_copy(c, i).wait_send()
    for i in range(1, NY):
        want_copy(i).wait_send()
    for way in range(2):
        far_want_copy(way).wait_send()
        sent = sum(kind == "send" and w == way and d < half - 1 for slot in order for kind, w, d, _ in slot)
        whole = ring.at[pl.ds(0, sent // nq)]
        pltpu.make_async_copy(whole, whole, z_send.at[way]).wait()
        if sent % nq:
            some = ring.at[0, pl.ds(0, sent % nq)]
            pltpu.make_async_copy(some, some, z_send.at[way]).wait()
    pltpu.make_async_copy(far_out, far_out, far_send).wait()
    whole = picked.at[:, pl.ds(1, NY - 1)]
    pltpu.make_async_copy(whole, whole, y_send).wait()

    for t in range(nt):
        total = share[t, core, x]
        for i in range(1, nx):
            pltpu.make_async_copy(share_x.at[t, i], share_x.at[t, i], fx_recv.at[t, i]).wait()
            total = total + share_x[t, i]
        out[t] = total

    for t in range(nt):
        fc_copy(t).wait_send()
        for i in range(1, nx):
            fx_copy(t, i).wait_send()


def shards(spectrum, bessel_table, interp_weights, need_owner, need_block):
    bands = lax.axis_size("band")
    nz = lax.axis_size("pair") // NY
    nx = bands // 2
    depth, radial = bessel_table.shape
    nb = spectrum.shape[1] // PB
    nt, nj, tri, local = interp_weights.shape
    nq = local // CH
    units = local // UNIT
    groups = nq // GROUP
    wide = GROUP * CH
    rows = tri // bands
    sizes = (nx, nz, nq, nb, nt, nj, tri)
    weights = jnp.swapaxes(interp_weights, 2, 3)
    dma = pltpu.SemaphoreType.DMA
    return pl.pallas_call(
        functools.partial(kernel, sizes),
        out_shape=jax.ShapeDtypeStruct((nt, rows, PB), F32),
        in_specs=[pl.BlockSpec(memory_space=pl.ANY)] * 5,
        out_specs=pl.BlockSpec(memory_space=pltpu.VMEM),
        scratch_shapes=[
            pltpu.SMEM(need_owner.shape, jnp.int32),
            pltpu.SMEM(need_block.shape, jnp.int32),
            pltpu.VMEM((depth, radial), BF16),
            pltpu.VMEM(spectrum.shape, BF16),
            pltpu.VMEM(weights.shape, BF16),
            pltpu.VMEM((units, 2, nx, UNIT, depth), BF16),
            pltpu.VMEM((groups, nt, tri, nj * wide), BF16),
            pltpu.VMEM((units, 2, nx, UNIT, nb * PB), F32),
            pltpu.VMEM((units, nx, UNIT, nb * PB), F32),
            pltpu.VMEM((nq, nx, CH, nb * PB), F32),
            pltpu.VMEM((nz, nq, nb, CH, PB), F32),
            pltpu.VMEM((3, nb, CH, PB), F32),
            pltpu.VMEM((groups, NY, nz * 2, wide, PB), F32),
            pltpu.VMEM((NY * nz * 2, wide, PB), F32),
            pltpu.VMEM((NY * nz * 2, wide, PB), F32),
            pltpu.VMEM((groups, nt, nj * wide, 2 * PB), BF16),
            pltpu.VMEM((nt, tri, PB), F32),
            pltpu.VMEM((nt, 2, nx, rows, PB), F32),
            pltpu.VMEM((nt, nx, rows, PB), F32),
            pltpu.VMEM((nt, nx, rows, PB), F32),
            pltpu.VMEM((NY, 8, PB), jnp.int32),
            pltpu.SMEM((NY, 8, PB), jnp.int32),
            pltpu.SMEM((nt * nj,), jnp.int32),
            pltpu.VMEM((2, NY, 8, PB), jnp.int32),
            pltpu.SMEM((2, NY, 8, PB), jnp.int32),
            pltpu.VMEM((nq, NY * 2, CH, PB), F32),
            pltpu.VMEM((nq, NY * 2, CH, PB), F32),
            dma((5,)),
            dma((units,)),
            dma((units,)),
            dma((nq, nx)),
            dma((nq, nx)),
            dma((2,)),
            dma((2, nz // 2 + 1, nq)),
            dma((NY,)),
            dma((NY,)),
            dma,
            dma,
            dma((groups,)),
            dma((2,)),
            dma((2,)),
            dma,
            dma,
            dma((nt,)),
            dma((nt,)),
            dma((nt, nx)),
            dma((nt, nx)),
        ],
        compiler_params=pltpu.CompilerParams(
            collective_id=0, has_side_effects=True, vmem_limit_bytes=56 * 1024 * 1024
        ),
        cost_estimate=pl.CostEstimate(flops=1 << 30, bytes_accessed=4 << 20, transcendentals=0),
    )(bessel_table, spectrum, weights, need_owner, need_block)


def solution(mesh):
    return jax.shard_map(
        shards,
        mesh=mesh,
        in_specs=(
            P("band", "pair"),
            P("band", None),
            P("pair", None, None, "band"),
            P("pair", None),
            P("pair", None),
        ),
        out_specs=P("pair", "band", None),
        check_vma=False,
    )
```

```python
import functools

import jax
import jax.numpy as jnp
from jax import lax
from jax.experimental import pallas as pl
from jax.experimental.pallas import tpu as pltpu
from jax.sharding import PartitionSpec as P

PB = 128
NY = 4
CH = 8
UNIT = 16
GROUP = 4
LAG = 5
LATE = 3
PACE = 2
AHEAD = 3
MESH = pl.DeviceIdType.MESH
F32 = jnp.float32
BF16 = jnp.bfloat16


def z_order(nz, nq):
    half = nz // 2
    ready = [{(0, c): PACE * c for c in range(nq)} for _ in range(2)]
    ends = [{}, {}]
    order, time = [], 0
    while any(ready) or any(ends):
        slot = []
        for way in range(2):
            now = [k for k, at in ready[way].items() if at <= time]
            if now:
                d, c = min(now, key=lambda k: (k[1] // GROUP, k[0], k[1]))
                del ready[way][d, c]
                slot.append(("send", way, d, c))
                goes_on = d + 1 < half - 1 or (d + 1 == half - 1 and c % 2 == way)
                (ready if goes_on else ends)[way][d + 1, c] = time + LAG
            for d, c in sorted(k for k, at in ends[way].items() if at <= time):
                del ends[way][d, c]
                slot.append(("end", way, d, c))
        order.append(slot)
        time += 1
    return order


def kernel(
    sizes,
    table_in, spec_in, weights_in, owner_hbm, block_hbm,
    out,
    owner_in, block_in,
    table, spec, weights, table_t, weights_t,
    part, core_in, band_in, ring, desk, picked, slots_0, slots_1, blocks, early,
    share, share_core, share_x,
    wants, wants_s, place_s, far_wants, far_s, far_out, far_in,
    load_sem, core_send, core_recv, x_send, x_recv, z_send, z_recv,
    want_send, want_recv, want_local, y_send, y_recv, fw_send, fw_recv, far_local, far_send,
    fc_send, fc_recv, fx_send, fx_recv,
):
    nx, nz, nq, nb, nt, nj, tri = sizes
    bands = 2 * nx
    half = nz // 2
    units = nq * CH // UNIT
    per_unit = UNIT // CH
    groups = nq // GROUP
    slots = (slots_0, slots_1)
    pair = lax.axis_index("pair")
    band = lax.axis_index("band")
    z, y = pair // NY, lax.rem(pair, NY)
    x, core = band // 2, lax.rem(band, 2)
    rows = tri // bands
    y_order = sorted(range(1, NY), key=lambda i: -min(i, NY - i))
    x_order = sorted(range(1, nx), key=lambda i: -min(i, nx - i))

    def x_peer(i):
        return (pair, lax.rem(x + i, nx) * 2 + core)

    def y_peer(i):
        return (z * NY + lax.rem(y + i, NY), band)

    sibling = (pair, x * 2 + 1 - core)
    up = (lax.rem(z + 1, nz) * NY + y, band)
    down = (lax.rem(z + nz - 1, nz) * NY + y, band)

    loads = [
        pltpu.make_async_copy(src, dst, load_sem.at[i])
        for i, (src, dst) in enumerate((
            (table_in, table), (spec_in, spec), (weights_in, weights),
            (owner_hbm, owner_in), (block_hbm, block_in),
        ))
    ]
    for i in (0, 1, 3, 4, 2):
        loads[i].start()

    barrier = pltpu.get_barrier_semaphore()
    partners = [x_peer(i) for i in range(1, nx)] + [y_peer(i) for i in range(1, NY)] + [up, down, sibling]
    for partner in partners:
        pl.semaphore_signal(barrier, inc=1, device_id=partner, device_id_type=MESH)

    loads[3].wait()
    loads[4].wait()
    lane = lax.broadcasted_iota(jnp.int32, (8, PB), 1)
    row = lax.broadcasted_iota(jnp.int32, (8, PB), 0)
    zero = jnp.zeros((8, PB), jnp.int32)

    def want_row(t, carry):
        first, second, count = carry
        for j in range(nj):
            hit = lane == owner_in[t, j]
            number = block_in[t, j]
            first = jnp.where(hit & (count == 0), number, first)
            second = jnp.where(hit & (count == 1), number, second)
            count = count + hit.astype(jnp.int32)
        return first, second, count

    first, second, _ = lax.fori_loop(0, nt, want_row, (zero, zero, zero))
    wants[0] = jnp.where(row == 0, first, jnp.where(row == 1, second, 0))

    loads[0].wait()
    turned = table[...].T
    for b in range(bands):
        for u in range(units):
            at = (b * units + u) * UNIT
            table_t[u, b % 2, b // 2] = turned[at : at + UNIT]
    loads[1].wait()

    def hankel(u):
        left = table_t[u].reshape(bands * UNIT, table_t.shape[-1])
        product = jnp.dot(left, spec[...], preferred_element_type=F32)
        part[u] = product.reshape(2, nx, UNIT, nb * PB)

    def core_copy(u):
        return pltpu.make_async_remote_copy(
            part.at[u, 1 - core], core_in.at[u], core_send.at[u], core_recv.at[u],
            device_id=sibling, device_id_type=MESH,
        )

    def x_copy(c, i):
        some = pl.ds(c % per_unit * CH, CH)
        return pltpu.make_async_remote_copy(
            part.at[c // per_unit, core, lax.rem(x + i, nx), some], band_in.at[c, nx - i],
            x_send.at[c, i], x_recv.at[c, nx - i],
            device_id=x_peer(i), device_id_type=MESH,
        )

    def x_start(c):
        for i in x_order:
            x_copy(c, i).start()

    def across_cores(u):
        core_copy(u).wait_recv()
        part[u, core] = part[u, core] + core_in[u]
        for c in range(u * per_unit, (u + 1) * per_unit):
            if c < AHEAD:
                x_start(c)

    def own_rows(c):
        for i in range(1, nx):
            pltpu.make_async_copy(band_in.at[c, i], band_in.at[c, i], x_recv.at[c, i]).wait()
        at = c % per_unit * CH
        total = part[c // per_unit, core, x, at : at + CH]
        for i in range(1, nx):
            total = total + band_in[c, i]
        for b in range(nb):
            ring[0, c, b] = total[:, b * PB : (b + 1) * PB]
        if c + AHEAD < nq:
            x_start(c + AHEAD)

    def want_copy(i):
        return pltpu.make_async_remote_copy(
            wants.at[0], wants.at[NY - i], want_send.at[i], want_recv.at[NY - i],
            device_id=y_peer(i), device_id_type=MESH,
        )

    hankel(0)
    pl.semaphore_wait(barrier, len(partners))
    core_copy(0).start()
    for i in range(1, NY):
        want_copy(i).start()
    for u in range(1, units):
        hankel(u)
        core_copy(u).start()
        across_cores(u - 1)
    across_cores(units - 1)

    to_scalar = pltpu.make_async_copy(wants, wants_s, want_local)
    for i in range(1, NY):
        pltpu.make_async_copy(wants.at[i], wants.at[i], want_recv.at[i]).wait()
    to_scalar.start()

    def far_want_copy(way):
        return pltpu.make_async_remote_copy(
            wants, far_wants.at[1 - way], fw_send.at[way], fw_recv.at[1 - way],
            device_id=up if way == 0 else down, device_id_type=MESH,
        )

    for way in range(2):
        far_want_copy(way).start()
    to_far = pltpu.make_async_copy(far_wants, far_s, far_local)

    def place_row(t):
        for j in range(nj):
            who = owner_in[t, j]
            rank = jnp.int32(0)
            for u in range(t):
                for k in range(nj):
                    rank = rank + (owner_in[u, k] == who).astype(jnp.int32)
            dz = lax.rem(z - who // NY + nz, nz)
            dy = lax.rem(lax.rem(who, NY) - y + NY, NY)
            place_s[t * nj + j] = (dy * nz + dz) * 2 + jnp.minimum(rank, 1)

    def turn(t):
        for g in range(groups):
            at = g * GROUP * CH
            some = weights[t, :, at : at + GROUP * CH, :]
            weights_t[g, t] = some.reshape(nj * GROUP * CH, tri).T

    def z_copy(way, d, c):
        here = d if way == 0 else (nz - d) % nz
        there = d + 1 if way == 0 else nz - d - 1
        return pltpu.make_async_remote_copy(
            ring.at[here, c], ring.at[there, c], z_send.at[way], z_recv.at[way, d + 1, c],
            device_id=up if way == 0 else down, device_id_type=MESH,
        )

    def z_wait(way, d, c):
        here = d if way == 0 else nz - d
        what = far_in.at[c] if d == half else ring.at[here, c]
        pltpu.make_async_copy(what, what, z_recv.at[way, d, c]).wait()

    def far_copy(way, c):
        return pltpu.make_async_remote_copy(
            far_out.at[c], far_in.at[c], far_send, z_recv.at[way, half, c],
            device_id=up if way == 0 else down, device_id_type=MESH,
        )

    def far_go(way, c):
        here = half - 1 if way == 0 else nz - half + 1
        desk[2] = ring[here, c]
        who = lax.rem(z + nz - here, nz) * NY + y
        for i in range(NY):
            for s in range(2):
                far_out[c, i * 2 + s] = desk[2, far_s[way, i, s, who]]
        far_copy(way, c).start()

    def far_come(c):
        g = c // GROUP
        at = c % GROUP * CH
        done[half, c] = True
        slots[g][half * 2 : half * 2 + 2, at : at + CH] = far_in[c, 0:2]
        for i in y_order:
            pltpu.make_async_remote_copy(
                far_in.at[c, pl.ds(i * 2, 2)],
                slots[g].at[pl.ds(((NY - i) * nz + half) * 2, 2), pl.ds(at, CH)],
                y_send, y_recv.at[g],
                device_id=y_peer(i), device_id_type=MESH,
            ).start()

    def y_copy(i, g, here, at, count):
        some = pl.ds(at, count)
        return pltpu.make_async_remote_copy(
            picked.at[g, i, pl.ds(here * 2, 2), some],
            slots[g].at[pl.ds(((NY - i) * nz + here) * 2, 2), some],
            y_send, y_recv.at[g],
            device_id=y_peer(i), device_id_type=MESH,
        )

    done = {}

    def pick(here, c):
        g = c // GROUP
        at = c % GROUP * CH
        n = len(done) % 2
        done[here, c] = True
        desk[n] = ring[here, c]
        who = lax.rem(z + nz - here, nz) * NY + y
        for i in range(NY):
            for s in range(2):
                rows_of = desk[n, wants_s[i, s, who]]
                if i == 0:
                    slots[g][here * 2 + s, at : at + CH] = rows_of
                else:
                    picked[g, i, here * 2 + s, at : at + CH] = rows_of
        if g == groups - 1 and abs(here - nz // 2) <= LATE:
            for i in y_order:
                y_copy(i, g, here, at, CH).start()
        elif all((here, k) in done for k in range(g * GROUP, (g + 1) * GROUP)):
            for i in y_order:
                y_copy(i, g, here, 0, GROUP * CH).start()

    def product(g, t):
        for j in range(nj):
            value = slots[g][place_s[t * nj + j]]
            high = value.astype(BF16)
            low = (value - high.astype(F32)).astype(BF16)
            at = j * GROUP * CH
            blocks[g, t, at : at + GROUP * CH, :PB] = high
            blocks[g, t, at : at + GROUP * CH, PB:] = low
        both = jnp.dot(weights_t[g, t], blocks[g, t], preferred_element_type=F32)
        return both[:, :PB] + both[:, PB:]

    def y_wait(g):
        whole = slots[g].at[pl.ds(nz * 2, (NY - 1) * nz * 2)]
        pltpu.make_async_copy(whole, whole, y_recv.at[g]).wait()

    def early_tile(g, t):
        total = product(g, t)
        early[t] = total if g == 0 else early[t] + total

    order = z_order(nz, nq)
    last_of, own, far_ready = {}, {}, []
    for n, slot in enumerate(order):
        for kind, way, d, c in slot:
            last_of[c // GROUP] = n
    lay_by = {min(last_of[g] + 8 + 2 * t, len(order) - 1 - nt + t): (g, t) for g in range(groups - 1) for t in range(nt)}
    set_up = {min(12 + 2 * t, len(order) - 1 - nt + t): t for t in range(nt)}
    for n, slot in enumerate(order):
        for kind, way, d, c in slot:
            if d:
                z_wait(way, d, c)
            elif c not in own:
                own_rows(c)
                own[c] = n
            if kind == "send" and d == half - 1:
                if not far_ready:
                    for w in range(2):
                        pltpu.make_async_copy(far_wants.at[w], far_wants.at[w], fw_recv.at[w]).wait()
                    to_far.start()
                    to_far.wait()
                    far_ready.append(n)
                far_go(way, c)
            elif kind == "send":
                z_copy(way, d, c).start()
        if n == 0:
            to_scalar.wait()
        for kind, way, d, c in slot:
            if d == half:
                far_come(c)
            elif (d if way == 0 else (nz - d) % nz, c) not in done:
                pick(d if way == 0 else (nz - d) % nz, c)
        if n in set_up:
            place_row(set_up[n])
            if set_up[n] == 0:
                loads[2].wait()
            turn(set_up[n])
        if n in lay_by:
            g, t = lay_by[n]
            if t == 0:
                y_wait(g)
            early_tile(g, t)

    def fc_copy(t):
        return pltpu.make_async_remote_copy(
            share.at[t, 1 - core], share_core.at[t], fc_send.at[t], fc_recv.at[t],
            device_id=sibling, device_id_type=MESH,
        )

    def fx_copy(t, i):
        return pltpu.make_async_remote_copy(
            share.at[t, core, lax.rem(x + i, nx)], share_x.at[t, nx - i],
            fx_send.at[t, i], fx_recv.at[t, nx - i],
            device_id=x_peer(i), device_id_type=MESH,
        )

    y_wait(groups - 1)

    for t in range(nt):
        total = product(groups - 1, t)
        if groups > 1:
            total = total + early[t]
        for b in range(bands):
            share[t, b % 2, b // 2] = total[b * rows : (b + 1) * rows]
        fc_copy(t).start()
    for t in range(nt):
        fc_copy(t).wait_recv()
        share[t, core] = share[t, core] + share_core[t]
        for i in x_order:
            fx_copy(t, i).start()
    for u in range(units):
        core_copy(u).wait_send()
    for c in range(nq):
        for i in range(1, nx):
            x_copy(c, i).wait_send()
    for i in range(1, NY):
        want_copy(i).wait_send()
    for way in range(2):
        far_want_copy(way).wait_send()
        sent = sum(kind == "send" and w == way and d < half - 1 for slot in order for kind, w, d, _ in slot)
        whole = ring.at[pl.ds(0, sent // nq)]
        pltpu.make_async_copy(whole, whole, z_send.at[way]).wait()
        if sent % nq:
            some = ring.at[0, pl.ds(0, sent % nq)]
            pltpu.make_async_copy(some, some, z_send.at[way]).wait()
    pltpu.make_async_copy(far_out, far_out, far_send).wait()
    whole = picked.at[:, pl.ds(1, NY - 1)]
    pltpu.make_async_copy(whole, whole, y_send).wait()

    for t in range(nt):
        total = share[t, core, x]
        for i in range(1, nx):
            pltpu.make_async_copy(share_x.at[t, i], share_x.at[t, i], fx_recv.at[t, i]).wait()
            total = total + share_x[t, i]
        out[t] = total

    for t in range(nt):
        fc_copy(t).wait_send()
        for i in range(1, nx):
            fx_copy(t, i).wait_send()


def shards(spectrum, bessel_table, interp_weights, need_owner, need_block):
    bands = lax.axis_size("band")
    nz = lax.axis_size("pair") // NY
    nx = bands // 2
    depth, radial = bessel_table.shape
    nb = spectrum.shape[1] // PB
    nt, nj, tri, local = interp_weights.shape
    nq = local // CH
    units = local // UNIT
    groups = nq // GROUP
    wide = GROUP * CH
    rows = tri // bands
    sizes = (nx, nz, nq, nb, nt, nj, tri)
    weights = jnp.swapaxes(interp_weights, 2, 3)
    dma = pltpu.SemaphoreType.DMA
    return pl.pallas_call(
        functools.partial(kernel, sizes),
        out_shape=jax.ShapeDtypeStruct((nt, rows, PB), F32),
        in_specs=[pl.BlockSpec(memory_space=pl.ANY)] * 5,
        out_specs=pl.BlockSpec(memory_space=pltpu.VMEM),
        scratch_shapes=[
            pltpu.SMEM(need_owner.shape, jnp.int32),
            pltpu.SMEM(need_block.shape, jnp.int32),
            pltpu.VMEM((depth, radial), BF16),
            pltpu.VMEM(spectrum.shape, BF16),
            pltpu.VMEM(weights.shape, BF16),
            pltpu.VMEM((units, 2, nx, UNIT, depth), BF16),
            pltpu.VMEM((groups, nt, tri, nj * wide), BF16),
            pltpu.VMEM((units, 2, nx, UNIT, nb * PB), F32),
            pltpu.VMEM((units, nx, UNIT, nb * PB), F32),
            pltpu.VMEM((nq, nx, CH, nb * PB), F32),
            pltpu.VMEM((nz, nq, nb, CH, PB), F32),
            pltpu.VMEM((3, nb, CH, PB), F32),
            pltpu.VMEM((groups, NY, nz * 2, wide, PB), F32),
            pltpu.VMEM((NY * nz * 2, wide, PB), F32),
            pltpu.VMEM((NY * nz * 2, wide, PB), F32),
            pltpu.VMEM((groups, nt, nj * wide, 2 * PB), BF16),
            pltpu.VMEM((nt, tri, PB), F32),
            pltpu.VMEM((nt, 2, nx, rows, PB), F32),
            pltpu.VMEM((nt, nx, rows, PB), F32),
            pltpu.VMEM((nt, nx, rows, PB), F32),
            pltpu.VMEM((NY, 8, PB), jnp.int32),
            pltpu.SMEM((NY, 8, PB), jnp.int32),
            pltpu.SMEM((nt * nj,), jnp.int32),
            pltpu.VMEM((2, NY, 8, PB), jnp.int32),
            pltpu.SMEM((2, NY, 8, PB), jnp.int32),
            pltpu.VMEM((nq, NY * 2, CH, PB), F32),
            pltpu.VMEM((nq, NY * 2, CH, PB), F32),
            dma((5,)),
            dma((units,)),
            dma((units,)),
            dma((nq, nx)),
            dma((nq, nx)),
            dma((2,)),
            dma((2, nz // 2 + 1, nq)),
            dma((NY,)),
            dma((NY,)),
            dma,
            dma,
            dma((groups,)),
            dma((2,)),
            dma((2,)),
            dma,
            dma,
            dma((nt,)),
            dma((nt,)),
            dma((nt, nx)),
            dma((nt, nx)),
        ],
        compiler_params=pltpu.CompilerParams(
            collective_id=0, has_side_effects=True, vmem_limit_bytes=56 * 1024 * 1024
        ),
        cost_estimate=pl.CostEstimate(flops=1 << 30, bytes_accessed=4 << 20, transcendentals=0),
    )(bessel_table, spectrum, weights, need_owner, need_block)


def solution(mesh):
    return jax.shard_map(
        shards,
        mesh=mesh,
        in_specs=(
            P("band", "pair"),
            P("band", None),
            P("pair", None, None, "band"),
            P("pair", None),
            P("pair", None),
        ),
        out_specs=P("pair", "band", None),
        check_vma=False,
    )
```

```python
import functools

import jax
import jax.numpy as jnp
from jax import lax
from jax.experimental import pallas as pl
from jax.experimental.pallas import tpu as pltpu
from jax.sharding import PartitionSpec as P

PB = 128
NY = 4
CH = 8
UNIT = 16
GROUP = 4
LAG = 6
LATE = 3
PACE = 2
AHEAD = 3
MESH = pl.DeviceIdType.MESH
F32 = jnp.float32
BF16 = jnp.bfloat16


def z_order(nz, nq):
    half = nz // 2
    ready = [{(0, c): PACE * c for c in range(nq)} for _ in range(2)]
    ends = [{}, {}]
    order, time = [], 0
    while any(ready) or any(ends):
        slot = []
        for way in range(2):
            now = [k for k, at in ready[way].items() if at <= time]
            if now:
                d, c = min(now, key=lambda k: (k[1] // GROUP, k[0], k[1]))
                del ready[way][d, c]
                slot.append(("send", way, d, c))
                goes_on = d + 1 < half - 1 or (d + 1 == half - 1 and c % 2 == way)
                (ready if goes_on else ends)[way][d + 1, c] = time + LAG
            for d, c in sorted(k for k, at in ends[way].items() if at <= time):
                del ends[way][d, c]
                slot.append(("end", way, d, c))
        order.append(slot)
        time += 1
    return order


def kernel(
    sizes,
    table_in, spec_in, weights_in, owner_hbm, block_hbm,
    out,
    owner_in, block_in,
    table, spec, weights, table_t, weights_t,
    part, core_in, band_in, ring, desk, picked, slots_0, slots_1, blocks, early,
    share, share_core, share_x,
    wants, wants_s, place_s, far_wants, far_s, far_out, far_in,
    load_sem, core_send, core_recv, x_send, x_recv, z_send, z_recv,
    want_send, want_recv, want_local, y_send, y_recv, fw_send, fw_recv, far_local, far_send,
    fc_send, fc_recv, fx_send, fx_recv,
):
    nx, nz, nq, nb, nt, nj, tri = sizes
    bands = 2 * nx
    half = nz // 2
    units = nq * CH // UNIT
    per_unit = UNIT // CH
    groups = nq // GROUP
    slots = (slots_0, slots_1)
    pair = lax.axis_index("pair")
    band = lax.axis_index("band")
    z, y = pair // NY, lax.rem(pair, NY)
    x, core = band // 2, lax.rem(band, 2)
    rows = tri // bands
    y_order = sorted(range(1, NY), key=lambda i: -min(i, NY - i))
    x_order = sorted(range(1, nx), key=lambda i: -min(i, nx - i))

    def x_peer(i):
        return (pair, lax.rem(x + i, nx) * 2 + core)

    def y_peer(i):
        return (z * NY + lax.rem(y + i, NY), band)

    sibling = (pair, x * 2 + 1 - core)
    up = (lax.rem(z + 1, nz) * NY + y, band)
    down = (lax.rem(z + nz - 1, nz) * NY + y, band)

    loads = [
        pltpu.make_async_copy(src, dst, load_sem.at[i])
        for i, (src, dst) in enumerate((
            (table_in, table), (spec_in, spec), (weights_in, weights),
            (owner_hbm, owner_in), (block_hbm, block_in),
        ))
    ]
    for i in (0, 1, 3, 4, 2):
        loads[i].start()

    barrier = pltpu.get_barrier_semaphore()
    partners = [x_peer(i) for i in range(1, nx)] + [y_peer(i) for i in range(1, NY)] + [up, down, sibling]
    for partner in partners:
        pl.semaphore_signal(barrier, inc=1, device_id=partner, device_id_type=MESH)

    loads[3].wait()
    loads[4].wait()
    lane = lax.broadcasted_iota(jnp.int32, (8, PB), 1)
    row = lax.broadcasted_iota(jnp.int32, (8, PB), 0)
    zero = jnp.zeros((8, PB), jnp.int32)

    def want_row(t, carry):
        first, second, count = carry
        for j in range(nj):
            hit = lane == owner_in[t, j]
            number = block_in[t, j]
            first = jnp.where(hit & (count == 0), number, first)
            second = jnp.where(hit & (count == 1), number, second)
            count = count + hit.astype(jnp.int32)
        return first, second, count

    first, second, _ = lax.fori_loop(0, nt, want_row, (zero, zero, zero))
    wants[0] = jnp.where(row == 0, first, jnp.where(row == 1, second, 0))

    loads[0].wait()
    turned = table[...].T
    for b in range(bands):
        for u in range(units):
            at = (b * units + u) * UNIT
            table_t[u, b % 2, b // 2] = turned[at : at + UNIT]
    loads[1].wait()

    def hankel(u):
        left = table_t[u].reshape(bands * UNIT, table_t.shape[-1])
        product = jnp.dot(left, spec[...], preferred_element_type=F32)
        part[u] = product.reshape(2, nx, UNIT, nb * PB)

    def core_copy(u):
        return pltpu.make_async_remote_copy(
            part.at[u, 1 - core], core_in.at[u], core_send.at[u], core_recv.at[u],
            device_id=sibling, device_id_type=MESH,
        )

    def x_copy(c, i):
        some = pl.ds(c % per_unit * CH, CH)
        return pltpu.make_async_remote_copy(
            part.at[c // per_unit, core, lax.rem(x + i, nx), some], band_in.at[c, nx - i],
            x_send.at[c, i], x_recv.at[c, nx - i],
            device_id=x_peer(i), device_id_type=MESH,
        )

    def x_start(c):
        for i in x_order:
            x_copy(c, i).start()

    def across_cores(u):
        core_copy(u).wait_recv()
        part[u, core] = part[u, core] + core_in[u]
        for c in range(u * per_unit, (u + 1) * per_unit):
            if c < AHEAD:
                x_start(c)

    def own_rows(c):
        for i in range(1, nx):
            pltpu.make_async_copy(band_in.at[c, i], band_in.at[c, i], x_recv.at[c, i]).wait()
        at = c % per_unit * CH
        total = part[c // per_unit, core, x, at : at + CH]
        for i in range(1, nx):
            total = total + band_in[c, i]
        for b in range(nb):
            ring[0, c, b] = total[:, b * PB : (b + 1) * PB]
        if c + AHEAD < nq:
            x_start(c + AHEAD)

    def want_copy(i):
        return pltpu.make_async_remote_copy(
            wants.at[0], wants.at[NY - i], want_send.at[i], want_recv.at[NY - i],
            device_id=y_peer(i), device_id_type=MESH,
        )

    hankel(0)
    pl.semaphore_wait(barrier, len(partners))
    core_copy(0).start()
    for i in range(1, NY):
        want_copy(i).start()
    for u in range(1, units):
        hankel(u)
        core_copy(u).start()
        across_cores(u - 1)
    across_cores(units - 1)

    to_scalar = pltpu.make_async_copy(wants, wants_s, want_local)
    for i in range(1, NY):
        pltpu.make_async_copy(wants.at[i], wants.at[i], want_recv.at[i]).wait()
    to_scalar.start()

    def far_want_copy(way):
        return pltpu.make_async_remote_copy(
            wants, far_wants.at[1 - way], fw_send.at[way], fw_recv.at[1 - way],
            device_id=up if way == 0 else down, device_id_type=MESH,
        )

    for way in range(2):
        far_want_copy(way).start()
    to_far = pltpu.make_async_copy(far_wants, far_s, far_local)

    def place_row(t):
        for j in range(nj):
            who = owner_in[t, j]
            rank = jnp.int32(0)
            for u in range(t):
                for k in range(nj):
                    rank = rank + (owner_in[u, k] == who).astype(jnp.int32)
            dz = lax.rem(z - who // NY + nz, nz)
            dy = lax.rem(lax.rem(who, NY) - y + NY, NY)
            place_s[t * nj + j] = (dy * nz + dz) * 2 + jnp.minimum(rank, 1)

    def turn(t):
        for g in range(groups):
            at = g * GROUP * CH
            some = weights[t, :, at : at + GROUP * CH, :]
            weights_t[g, t] = some.reshape(nj * GROUP * CH, tri).T

    def z_copy(way, d, c):
        here = d if way == 0 else (nz - d) % nz
        there = d + 1 if way == 0 else nz - d - 1
        return pltpu.make_async_remote_copy(
            ring.at[here, c], ring.at[there, c], z_send.at[way], z_recv.at[way, d + 1, c],
            device_id=up if way == 0 else down, device_id_type=MESH,
        )

    def z_wait(way, d, c):
        here = d if way == 0 else nz - d
        what = far_in.at[c] if d == half else ring.at[here, c]
        pltpu.make_async_copy(what, what, z_recv.at[way, d, c]).wait()

    def far_copy(way, c):
        return pltpu.make_async_remote_copy(
            far_out.at[c], far_in.at[c], far_send, z_recv.at[way, half, c],
            device_id=up if way == 0 else down, device_id_type=MESH,
        )

    def far_go(way, c):
        here = half - 1 if way == 0 else nz - half + 1
        desk[2] = ring[here, c]
        who = lax.rem(z + nz - here, nz) * NY + y
        for i in range(NY):
            for s in range(2):
                far_out[c, i * 2 + s] = desk[2, far_s[way, i, s, who]]
        far_copy(way, c).start()

    def far_come(c):
        g = c // GROUP
        at = c % GROUP * CH
        done[half, c] = True
        slots[g][half * 2 : half * 2 + 2, at : at + CH] = far_in[c, 0:2]
        for i in y_order:
            pltpu.make_async_remote_copy(
                far_in.at[c, pl.ds(i * 2, 2)],
                slots[g].at[pl.ds(((NY - i) * nz + half) * 2, 2), pl.ds(at, CH)],
                y_send, y_recv.at[g],
                device_id=y_peer(i), device_id_type=MESH,
            ).start()

    def y_copy(i, g, here, at, count):
        some = pl.ds(at, count)
        return pltpu.make_async_remote_copy(
            picked.at[g, i, pl.ds(here * 2, 2), some],
            slots[g].at[pl.ds(((NY - i) * nz + here) * 2, 2), some],
            y_send, y_recv.at[g],
            device_id=y_peer(i), device_id_type=MESH,
        )

    done = {}

    def pick(here, c):
        g = c // GROUP
        at = c % GROUP * CH
        n = len(done) % 2
        done[here, c] = True
        desk[n] = ring[here, c]
        who = lax.rem(z + nz - here, nz) * NY + y
        for i in range(NY):
            for s in range(2):
                rows_of = desk[n, wants_s[i, s, who]]
                if i == 0:
                    slots[g][here * 2 + s, at : at + CH] = rows_of
                else:
                    picked[g, i, here * 2 + s, at : at + CH] = rows_of
        if g == groups - 1 and abs(here - nz // 2) <= LATE:
            for i in y_order:
                y_copy(i, g, here, at, CH).start()
        elif all((here, k) in done for k in range(g * GROUP, (g + 1) * GROUP)):
            for i in y_order:
                y_copy(i, g, here, 0, GROUP * CH).start()

    def product(g, t):
        for j in range(nj):
            value = slots[g][place_s[t * nj + j]]
            high = value.astype(BF16)
            low = (value - high.astype(F32)).astype(BF16)
            at = j * GROUP * CH
            blocks[g, t, at : at + GROUP * CH, :PB] = high
            blocks[g, t, at : at + GROUP * CH, PB:] = low
        both = jnp.dot(weights_t[g, t], blocks[g, t], preferred_element_type=F32)
        return both[:, :PB] + both[:, PB:]

    def y_wait(g):
        whole = slots[g].at[pl.ds(nz * 2, (NY - 1) * nz * 2)]
        pltpu.make_async_copy(whole, whole, y_recv.at[g]).wait()

    def early_tile(g, t):
        total = product(g, t)
        early[t] = total if g == 0 else early[t] + total

    order = z_order(nz, nq)
    last_of, own, far_ready = {}, {}, []
    for n, slot in enumerate(order):
        for kind, way, d, c in slot:
            last_of[c // GROUP] = n
    lay_by = {min(last_of[g] + 8 + 2 * t, len(order) - 1 - nt + t): (g, t) for g in range(groups - 1) for t in range(nt)}
    set_up = {min(12 + 2 * t, len(order) - 1 - nt + t): t for t in range(nt)}
    for n, slot in enumerate(order):
        for kind, way, d, c in slot:
            if d:
                z_wait(way, d, c)
            elif c not in own:
                own_rows(c)
                own[c] = n
            if kind == "send" and d == half - 1:
                if not far_ready:
                    for w in range(2):
                        pltpu.make_async_copy(far_wants.at[w], far_wants.at[w], fw_recv.at[w]).wait()
                    to_far.start()
                    to_far.wait()
                    far_ready.append(n)
                far_go(way, c)
            elif kind == "send":
                z_copy(way, d, c).start()
        if n == 0:
            to_scalar.wait()
        for kind, way, d, c in slot:
            if d == half:
                far_come(c)
            elif (d if way == 0 else (nz - d) % nz, c) not in done:
                pick(d if way == 0 else (nz - d) % nz, c)
        if n in set_up:
            place_row(set_up[n])
            if set_up[n] == 0:
                loads[2].wait()
            turn(set_up[n])
        if n in lay_by:
            g, t = lay_by[n]
            if t == 0:
                y_wait(g)
            early_tile(g, t)

    def fc_copy(t):
        return pltpu.make_async_remote_copy(
            share.at[t, 1 - core], share_core.at[t], fc_send.at[t], fc_recv.at[t],
            device_id=sibling, device_id_type=MESH,
        )

    def fx_copy(t, i):
        return pltpu.make_async_remote_copy(
            share.at[t, core, lax.rem(x + i, nx)], share_x.at[t, nx - i],
            fx_send.at[t, i], fx_recv.at[t, nx - i],
            device_id=x_peer(i), device_id_type=MESH,
        )

    y_wait(groups - 1)

    for t in range(nt):
        total = product(groups - 1, t)
        if groups > 1:
            total = total + early[t]
        for b in range(bands):
            share[t, b % 2, b // 2] = total[b * rows : (b + 1) * rows]
        fc_copy(t).start()
    for t in range(nt):
        fc_copy(t).wait_recv()
        share[t, core] = share[t, core] + share_core[t]
        for i in x_order:
            fx_copy(t, i).start()
    for u in range(units):
        core_copy(u).wait_send()
    for c in range(nq):
        for i in range(1, nx):
            x_copy(c, i).wait_send()
    for i in range(1, NY):
        want_copy(i).wait_send()
    for way in range(2):
        far_want_copy(way).wait_send()
        sent = sum(kind == "send" and w == way and d < half - 1 for slot in order for kind, w, d, _ in slot)
        whole = ring.at[pl.ds(0, sent // nq)]
        pltpu.make_async_copy(whole, whole, z_send.at[way]).wait()
        if sent % nq:
            some = ring.at[0, pl.ds(0, sent % nq)]
            pltpu.make_async_copy(some, some, z_send.at[way]).wait()
    pltpu.make_async_copy(far_out, far_out, far_send).wait()
    whole = picked.at[:, pl.ds(1, NY - 1)]
    pltpu.make_async_copy(whole, whole, y_send).wait()

    for t in range(nt):
        total = share[t, core, x]
        for i in range(1, nx):
            pltpu.make_async_copy(share_x.at[t, i], share_x.at[t, i], fx_recv.at[t, i]).wait()
            total = total + share_x[t, i]
        out[t] = total

    for t in range(nt):
        fc_copy(t).wait_send()
        for i in range(1, nx):
            fx_copy(t, i).wait_send()


def shards(spectrum, bessel_table, interp_weights, need_owner, need_block):
    bands = lax.axis_size("band")
    nz = lax.axis_size("pair") // NY
    nx = bands // 2
    depth, radial = bessel_table.shape
    nb = spectrum.shape[1] // PB
    nt, nj, tri, local = interp_weights.shape
    nq = local // CH
    units = local // UNIT
    groups = nq // GROUP
    wide = GROUP * CH
    rows = tri // bands
    sizes = (nx, nz, nq, nb, nt, nj, tri)
    weights = jnp.swapaxes(interp_weights, 2, 3)
    dma = pltpu.SemaphoreType.DMA
    return pl.pallas_call(
        functools.partial(kernel, sizes),
        out_shape=jax.ShapeDtypeStruct((nt, rows, PB), F32),
        in_specs=[pl.BlockSpec(memory_space=pl.ANY)] * 5,
        out_specs=pl.BlockSpec(memory_space=pltpu.VMEM),
        scratch_shapes=[
            pltpu.SMEM(need_owner.shape, jnp.int32),
            pltpu.SMEM(need_block.shape, jnp.int32),
            pltpu.VMEM((depth, radial), BF16),
            pltpu.VMEM(spectrum.shape, BF16),
            pltpu.VMEM(weights.shape, BF16),
            pltpu.VMEM((units, 2, nx, UNIT, depth), BF16),
            pltpu.VMEM((groups, nt, tri, nj * wide), BF16),
            pltpu.VMEM((units, 2, nx, UNIT, nb * PB), F32),
            pltpu.VMEM((units, nx, UNIT, nb * PB), F32),
            pltpu.VMEM((nq, nx, CH, nb * PB), F32),
            pltpu.VMEM((nz, nq, nb, CH, PB), F32),
            pltpu.VMEM((3, nb, CH, PB), F32),
            pltpu.VMEM((groups, NY, nz * 2, wide, PB), F32),
            pltpu.VMEM((NY * nz * 2, wide, PB), F32),
            pltpu.VMEM((NY * nz * 2, wide, PB), F32),
            pltpu.VMEM((groups, nt, nj * wide, 2 * PB), BF16),
            pltpu.VMEM((nt, tri, PB), F32),
            pltpu.VMEM((nt, 2, nx, rows, PB), F32),
            pltpu.VMEM((nt, nx, rows, PB), F32),
            pltpu.VMEM((nt, nx, rows, PB), F32),
            pltpu.VMEM((NY, 8, PB), jnp.int32),
            pltpu.SMEM((NY, 8, PB), jnp.int32),
            pltpu.SMEM((nt * nj,), jnp.int32),
            pltpu.VMEM((2, NY, 8, PB), jnp.int32),
            pltpu.SMEM((2, NY, 8, PB), jnp.int32),
            pltpu.VMEM((nq, NY * 2, CH, PB), F32),
            pltpu.VMEM((nq, NY * 2, CH, PB), F32),
            dma((5,)),
            dma((units,)),
            dma((units,)),
            dma((nq, nx)),
            dma((nq, nx)),
            dma((2,)),
            dma((2, nz // 2 + 1, nq)),
            dma((NY,)),
            dma((NY,)),
            dma,
            dma,
            dma((groups,)),
            dma((2,)),
            dma((2,)),
            dma,
            dma,
            dma((nt,)),
            dma((nt,)),
            dma((nt, nx)),
            dma((nt, nx)),
        ],
        compiler_params=pltpu.CompilerParams(
            collective_id=0, has_side_effects=True, vmem_limit_bytes=56 * 1024 * 1024
        ),
        cost_estimate=pl.CostEstimate(flops=1 << 30, bytes_accessed=4 << 20, transcendentals=0),
    )(bessel_table, spectrum, weights, need_owner, need_block)


def solution(mesh):
    return jax.shard_map(
        shards,
        mesh=mesh,
        in_specs=(
            P("band", "pair"),
            P("band", None),
            P("pair", None, None, "band"),
            P("pair", None),
            P("pair", None),
        ),
        out_specs=P("pair", "band", None),
        check_vma=False,
    )
```
